512 devices in a mesh: fsdp: 32 (over x_hi, z), seq: 16 (over y, x_lo, core).
Axes of the slice: x: 4 (x_hi: 2, x_lo: 2; x = x_hi * 2 + x_lo), y: 4, z: 16, core: 2. Of those that a mesh axis runs over, the one named last changes fastest.
Arguments:
- tokens: bfloat16 [2048, 4096], P('seq', 'fsdp'), may hold values from -6 to 6
- out_grad: bfloat16 [2048, 4096], P('seq', 'fsdp'), may hold values from -0.00390625 to 0.00390625
- loss_mask: int32 [2048], P('seq'), may hold values 0 or 1
- w_in0: bfloat16 [10240, 4096], P('fsdp', 'seq'), may hold values from -0.09375 to 0.09375
- w_in1: bfloat16 [10240, 4096], P('fsdp', 'seq'), may hold values from -0.09375 to 0.09375
- w_out: bfloat16 [10240, 4096], P('fsdp', 'seq'), may hold values from -0.0625 to 0.0625
- tan_in0: bfloat16 [2, 10240, 4096], P(None, 'fsdp', 'seq'), may hold values from -0.09375 to 0.09375
- tan_in1: bfloat16 [2, 10240, 4096], P(None, 'fsdp', 'seq'), may hold values from -0.09375 to 0.09375
- tan_out: bfloat16 [2, 10240, 4096], P(None, 'fsdp', 'seq'), may hold values from -0.0625 to 0.0625
Outputs:
- block_out: bfloat16 [2048, 4096], P('seq', 'fsdp')
- projection: float32 [4, 2], replicated
The draws below stay inside these ranges and needn't reach their ends.
All inputs are finite; a program needn't handle non-finite values. No bound on the sum of `loss_mask` on one device may be relied on, other than what follows from the above.
Results may differ from the reference program's by a relative error of at most 0.0049.
Values may be sent and summed in bfloat16 or wider, within the bound.
No kernel may reach another device: no remote copies, remote signals or barrier semaphores. Data moves between devices by JAX's collectives and lax.ppermute only.
A program may use at most 128 MiB of HBM per device.

```python
import math
import jax
import jax.numpy as jnp
from jax import lax

D = 4096
FF = 10240
K = 2
EXAMPLES = 4
TOKENS = 2048
LEN = 512


def place_ends(array, key, low, high):
    shape = array.shape
    index_at = [jax.random.randint(jax.random.fold_in(key, axis), (), 0, shape[axis]) for axis in range(len(shape))]
    array = array.at[tuple(index_at)].set(low)
    longest = shape.index(max(shape))
    index_at[longest] = (index_at[longest] + 1) % shape[longest]
    return array.at[tuple(index_at)].set(high)


def block_levels(rng, extent, split, smallest, high):
    level = 1.0
    for axis_at, blocks in split:
        heights = jax.random.uniform(jax.random.fold_in(jax.random.fold_in(rng, 6), axis_at), (blocks,), jnp.float32, smallest / len(split), high / len(split))
        level = level * jnp.repeat(jnp.exp(heights), extent[axis_at] // blocks).reshape((-1,) + (1,) * (len(extent) - 1 - axis_at))
    return level


def gaussian(rng, shape, deviation, most, cuts=(), kind=jnp.bfloat16):
    array = deviation * jax.random.normal(rng, shape, jnp.float32)
    if cuts:
        array = array * block_levels(rng, shape, cuts, -0.22, 0.18)
    return jnp.clip(array, -most, most).astype(kind)


def setup_inputs(seed: int = 0) -> dict:
    seeds = jax.random.split(jax.random.key(seed), 10)
    tokens = gaussian(seeds[0], (TOKENS, D), 1.0, 6.0, ((0, 16), (1, 32)))
    out_grad = gaussian(seeds[1], (TOKENS, D), (D * LEN) ** -0.5, 0.00390625, ((0, 16), (1, 32)))
    loss_mask = place_ends((jax.random.randint(seeds[2], (TOKENS,), 0, 4) < 3).astype(jnp.int32), jax.random.fold_in(seeds[2], 1), 0, 1)
    w_in0 = gaussian(seeds[3], (FF, D), D ** -0.5, 0.09375, ((0, 32), (1, 16)))
    w_in1 = gaussian(seeds[4], (FF, D), D ** -0.5, 0.09375, ((0, 32), (1, 16)))
    w_out = gaussian(seeds[5], (FF, D), FF ** -0.5, 0.0625, ((0, 32), (1, 16)))
    tan_in0 = gaussian(seeds[6], (K, FF, D), D ** -0.5, 0.09375, ((1, 32), (2, 16)))
    tan_in1 = gaussian(seeds[7], (K, FF, D), D ** -0.5, 0.09375, ((1, 32), (2, 16)))
    tan_out = gaussian(seeds[8], (K, FF, D), FF ** -0.5, 0.0625, ((1, 32), (2, 16)))
    return {"tokens": tokens, "out_grad": out_grad, "loss_mask": loss_mask, "w_in0": w_in0, "w_in1": w_in1, "w_out": w_out, "tan_in0": tan_in0, "tan_in1": tan_in1, "tan_out": tan_out}


def gelu_value_slope(value):
    coeff = math.sqrt(2.0 / math.pi)
    inner = coeff * (value + 0.044715 * value * value * value)
    tangent = jnp.tanh(inner)
    act = 0.5 * value * (1.0 + tangent)
    slope = 0.5 * (1.0 + tangent) + 0.5 * value * (1.0 - tangent * tangent) * coeff * (1.0 + 3.0 * 0.044715 * value * value)
    return (act, slope)

def reference(tokens, out_grad, loss_mask, w_in0, w_in1, w_out, tan_in0, tan_in1, tan_out):
    gate = jnp.dot(tokens, w_in0.T, preferred_element_type=jnp.float32)
    upper = jnp.dot(tokens, w_in1.T, preferred_element_type=jnp.float32)
    act, slope = gelu_value_slope(gate)
    hidden = (act * upper).astype(jnp.bfloat16)
    block_out = jnp.dot(hidden, w_out, preferred_element_type=jnp.float32).astype(jnp.bfloat16)
    grad32 = out_grad.astype(jnp.float32)
    columns = []
    for direction in range(K):
        gate_tan = jnp.dot(tokens, tan_in0[direction].T, preferred_element_type=jnp.float32)
        upper_tan = jnp.dot(tokens, tan_in1[direction].T, preferred_element_type=jnp.float32)
        hidden_tan = (slope * gate_tan * upper + act * upper_tan).astype(jnp.bfloat16)
        out_tan = jnp.dot(hidden_tan, w_out, preferred_element_type=jnp.float32) + jnp.dot(hidden, tan_out[direction], preferred_element_type=jnp.float32)
        columns.append(lax.optimization_barrier(jnp.sum(grad32 * out_tan, axis=1)))
    row_dots = jnp.stack(columns, axis=1)
    example_of = jnp.arange(TOKENS, dtype=jnp.int32) // LEN
    select = (example_of[:, None] == jnp.arange(EXAMPLES, dtype=jnp.int32)[None, :]).astype(jnp.float32)
    select = select * loss_mask.astype(jnp.float32)[:, None]
    projection = jnp.dot(select.T, row_dots, precision=lax.Precision.HIGHEST)
    return (block_out, projection)
```

```python
import functools
import math

import jax
import jax.numpy as jnp
from jax import lax
from jax.experimental import pallas as pl
from jax.experimental.pallas import tpu as pltpu
from jax.sharding import PartitionSpec as P

EXAMPLES = 4
F32 = jnp.float32
BF16 = jnp.bfloat16
NT = (((1,), (1,)), ((), ()))

X_PAIRS = [[i, i + 16] for i in range(16)]
Z_NEAR = [[h * 16 + q * 4 + r for r in range(4)] for h in range(2) for q in range(4)]
Z_FAR = [[h * 16 + q * 4 + r for q in range(4)] for h in range(2) for r in range(4)]
Z_ALL = [list(range(16)), list(range(16, 32))]


def gelu_value_slope(value):
    coeff = math.sqrt(2.0 / math.pi)
    inner = coeff * (value + 0.044715 * value * value * value)
    tangent = jnp.tanh(inner)
    act = 0.5 * value * (1.0 + tangent)
    slope = 0.5 * (1.0 + tangent) + 0.5 * value * (1.0 - tangent * tangent) * coeff * (
        1.0 + 3.0 * 0.044715 * value * value
    )
    return (act, slope)


def z_shift(array, step):
    perm = [(h * 16 + (z + step) % 16, h * 16 + z) for h in range(2) for z in range(16)]
    return lax.ppermute(array, "fsdp", perm)


def contract_blocks(place, parts, weights, counts):
    x_hi, z_lo = place[0], place[1]
    sums = [None] * len(counts)
    for shift in range(4):
        near = (z_lo + shift) % 4
        lanes = pl.ds(pl.multiple_of((near % 2) * 128, 128), 128)
        for other in range(2):
            row = jnp.bitwise_xor(x_hi, other)
            for at, which in enumerate(counts):
                term = lax.dot_general(
                    parts[which][shift](other),
                    weights[row, 0, near // 2, at, :, lanes],
                    NT,
                    preferred_element_type=F32,
                )
                sums[at] = term if sums[at] is None else sums[at] + term
    return sums


def readers(own, plus, minus, two_x, two_g):
    def full(ref, which):
        return lambda other: ref[0, other, which]

    def single(ref):
        return lambda other: ref[0, other]

    return [
        [full(own, 0), full(plus, 0), single(two_x), full(minus, 0)],
        [full(own, 1), full(plus, 1), single(two_g), full(minus, 1)],
    ]


def primal_kernel(
    place, own, plus, minus, two_x, two_g, weights, hidden, act_out, factor_out, dh_out, sums
):
    step = pl.program_id(0)
    terms = contract_blocks(
        place, readers(own, plus, minus, two_x, two_g), weights, (0, 0, 1)
    )

    @pl.when(step == 0)
    def _():
        for at in range(3):
            sums[at] = terms[at]

    @pl.when(step > 0)
    def _():
        for at in range(3):
            sums[at] += terms[at]

    @pl.when(step == pl.num_programs(0) - 1)
    def _():
        upper = sums[1]
        act, slope = gelu_value_slope(sums[0])
        hidden[...] = (act * upper).astype(BF16)
        act_out[...] = act
        factor_out[...] = slope * upper
        dh_out[...] = sums[2]


def output_kernel(hidden, weights, out):
    for at in range(weights.shape[0]):
        value = jnp.dot(hidden[...], weights[at, 0], preferred_element_type=F32)
        out[2 * at] = value[:, :128]
        out[2 * at + 1] = value[:, 128:]


def tangent_kernel(
    place, own, plus, minus, two_x, two_g, weights, hidden, act, factor, dh, mask, out, sums
):
    step = pl.program_id(0)
    terms = contract_blocks(
        place, readers(own, plus, minus, two_x, two_g), weights, (0, 0, 0, 0, 1, 1)
    )

    @pl.when(step == 0)
    def _():
        for at in range(6):
            sums[at] = terms[at]

    @pl.when(step > 0)
    def _():
        for at in range(6):
            sums[at] += terms[at]

    @pl.when(step == pl.num_programs(0) - 1)
    def _():
        rows = lax.broadcasted_iota(jnp.int32, (8, 128), 0)
        lanes = lax.broadcasted_iota(jnp.int32, (8, 128), 1)
        total = jnp.zeros((8, 128), F32)
        for k in range(2):
            tangent = (factor[...] * sums[k] + act[...] * sums[2 + k]).astype(BF16)
            value = tangent.astype(F32) * dh[...] + hidden[...].astype(F32) * sums[4 + k]
            value = jnp.sum(value, axis=1, keepdims=True) * mask[...]
            value = jnp.sum(value, axis=0, keepdims=True)
            total = jnp.where((rows == place[2]) & (lanes == k), value, total)
        out[...] = total


def activation_specs():
    full = pl.BlockSpec((1, 2, 2, 128, 128), lambda s, p: (s, 0, 0, 0, 0))
    single = pl.BlockSpec((1, 2, 128, 128), lambda s, p: (s, 0, 0, 0))
    return [full, full, full, single, single]


def whole(shape):
    return pl.BlockSpec(shape, lambda s, p: (0,) * len(shape))


def weight_spec(count):
    return pl.BlockSpec((2, 1, 2, count, 320, 256), lambda s, p: (0, s, 0, 0, 0, 0))


def shards(tokens, out_grad, loss_mask, w_in0, w_in1, w_out, tan_in0, tan_in1, tan_out):
    fsdp = lax.axis_index("fsdp")
    seq = lax.axis_index("seq")
    rows = tokens.shape[0]
    length = rows * lax.axis_size("seq") // EXAMPLES
    place = jnp.stack([fsdp // 16, fsdp % 4, seq * rows // length]).astype(jnp.int32)

    stack_w = jnp.stack([w_in0, w_in1, w_out])
    stack_t = jnp.concatenate([tan_in0, tan_in1, tan_out], axis=0)
    stack_t, stack_w = lax.optimization_barrier((stack_t, stack_w))
    full_w = lax.all_gather(stack_w, "seq", axis=0).reshape(2, 4, 2, 3, 320, 256)
    full_t = lax.all_gather(stack_t, "seq", axis=0).reshape(2, 4, 2, 6, 320, 256)

    both = jnp.stack([tokens, out_grad])
    other = lax.ppermute(both, "fsdp", [(i, (i + 16) % 32) for i in range(32)])
    own = lax.all_gather(jnp.stack([both, other]), "fsdp", axis=0, axis_index_groups=Z_FAR)
    plus = z_shift(own, 1)
    minus = z_shift(own, -1)
    two_x = z_shift(own[:, :, 0], 2)
    two_g = z_shift(own[:, :, 1], -2)
    acts = (own, plus, minus, two_x, two_g)

    flat = jax.ShapeDtypeStruct((128, 320), F32)
    hidden, act, factor, dh = pl.pallas_call(
        primal_kernel,
        out_shape=(jax.ShapeDtypeStruct((128, 320), BF16), flat, flat, flat),
        grid_spec=pltpu.PrefetchScalarGridSpec(
            num_scalar_prefetch=1,
            grid=(4,),
            in_specs=activation_specs() + [weight_spec(3)],
            out_specs=(whole((128, 320)),) * 4,
            scratch_shapes=[pltpu.VMEM((3, 128, 320), F32)],
        ),
        compiler_params=pltpu.CompilerParams(vmem_limit_bytes=32 * 2**20),
        cost_estimate=pl.CostEstimate(
            flops=2 * 3 * 128 * 320 * 4096, bytes_accessed=10 * 2**20, transcendentals=40960
        ),
        name="primal",
    )(place, *acts, full_w)

    partial = pl.pallas_call(
        output_kernel,
        out_shape=jax.ShapeDtypeStruct((32, 128, 128), F32),
        grid=(4,),
        in_specs=[
            pl.BlockSpec((128, 320), lambda s: (0, 0)),
            pl.BlockSpec((4, 1, 320, 256), lambda s: (s, 2, 0, 0)),
        ],
        out_specs=pl.BlockSpec((8, 128, 128), lambda s: (s, 0, 0)),
        compiler_params=pltpu.CompilerParams(vmem_limit_bytes=32 * 2**20),
        cost_estimate=pl.CostEstimate(
            flops=2 * 128 * 320 * 4096, bytes_accessed=5 * 2**20, transcendentals=0
        ),
        name="block_sums",
    )(hidden, full_w.reshape(16, 3, 320, 256))

    part = partial.reshape(2, 4, 4, 128, 128)
    part = jnp.sum(lax.all_to_all(part, "fsdp", 0, 0, axis_index_groups=X_PAIRS), axis=0)
    part = jnp.swapaxes(part, 0, 1)
    part = jnp.sum(lax.all_to_all(part, "fsdp", 0, 0, axis_index_groups=Z_NEAR), axis=0)
    part = jnp.sum(lax.all_to_all(part, "fsdp", 0, 0, axis_index_groups=Z_FAR), axis=0)
    block_out = part.astype(BF16)

    terms = pl.pallas_call(
        tangent_kernel,
        out_shape=jax.ShapeDtypeStruct((8, 128), F32),
        grid_spec=pltpu.PrefetchScalarGridSpec(
            num_scalar_prefetch=1,
            grid=(4,),
            in_specs=activation_specs()
            + [weight_spec(6)]
            + [whole((128, 320))] * 4
            + [whole((128, 1))],
            out_specs=whole((8, 128)),
            scratch_shapes=[pltpu.VMEM((6, 128, 320), F32)],
        ),
        compiler_params=pltpu.CompilerParams(vmem_limit_bytes=40 * 2**20),
        cost_estimate=pl.CostEstimate(
            flops=2 * 6 * 128 * 320 * 4096, bytes_accessed=18 * 2**20, transcendentals=0
        ),
        name="tangents",
    )(place, *acts, full_t, hidden, act, factor, dh, loss_mask.astype(F32)[:, None])

    def gather_sum(value, axis, groups, size):
        copies = jnp.broadcast_to(value[None], (size,) + value.shape)
        got = lax.all_to_all(copies, axis, 0, 0, axis_index_groups=groups)
        return jnp.sum(got, axis=0)

    terms = gather_sum(terms, "fsdp", Z_ALL, 16)
    terms = gather_sum(terms, "fsdp", X_PAIRS, 2)
    terms = gather_sum(terms, "seq", None, 16)
    return (block_out, terms[:EXAMPLES, :2])


def solution(mesh):
    placed = (
        P("seq", "fsdp"),
        P("seq", "fsdp"),
        P("seq"),
        P("fsdp", "seq"),
        P("fsdp", "seq"),
        P("fsdp", "seq"),
        P(None, "fsdp", "seq"),
        P(None, "fsdp", "seq"),
        P(None, "fsdp", "seq"),
    )
    return jax.shard_map(
        shards, mesh=mesh, in_specs=placed, out_specs=(P("seq", "fsdp"), P()), check_vma=False
    )
```

```python
import functools
import math

import jax
import jax.numpy as jnp
from jax import lax
from jax.experimental import pallas as pl
from jax.experimental.pallas import tpu as pltpu
from jax.sharding import PartitionSpec as P

EXAMPLES = 4
F32 = jnp.float32
BF16 = jnp.bfloat16
NT = (((1,), (1,)), ((), ()))

X_PAIRS = [[i, i + 16] for i in range(16)]
Z_NEAR = [[h * 16 + q * 4 + r for r in range(4)] for h in range(2) for q in range(4)]
Z_FAR = [[h * 16 + q * 4 + r for q in range(4)] for h in range(2) for r in range(4)]
Z_ALL = [list(range(16)), list(range(16, 32))]


def gelu_value_slope(value):
    coeff = math.sqrt(2.0 / math.pi)
    inner = coeff * (value + 0.044715 * value * value * value)
    tangent = jnp.tanh(inner)
    act = 0.5 * value * (1.0 + tangent)
    slope = 0.5 * (1.0 + tangent) + 0.5 * value * (1.0 - tangent * tangent) * coeff * (
        1.0 + 3.0 * 0.044715 * value * value
    )
    return (act, slope)


def z_shift(array, step):
    perm = [(h * 16 + (z + step) % 16, h * 16 + z) for h in range(2) for z in range(16)]
    return lax.ppermute(array, "fsdp", perm)


def pairs(place, own, plus, minus, two, which):
    x_hi, z_lo = place[0], place[1]
    found = []
    for other in range(2):
        held = [own[0, other, which], plus[0, other, which], two[0, other], minus[0, other, which]]
        near = []
        for at in range(4):
            block = held[0]
            for shift in range(1, 4):
                block = jnp.where((z_lo + shift) % 4 == at, held[shift], block)
            near.append(block)
        row = jnp.bitwise_xor(x_hi, other)
        for half in range(2):
            block = jnp.concatenate([near[2 * half], near[2 * half + 1]], axis=1)
            found.append((row, half, block))
    return found


def contract(blocks, weights, first, count):
    total = None
    for row, half, block in blocks:
        rows = weights[row, 0, half, first : first + count].reshape(count * 320, 256)
        term = lax.dot_general(block, rows, NT, preferred_element_type=F32)
        total = term if total is None else total + term
    return total


def add_up(step, sums, term):
    @pl.when(step == 0)
    def _():
        sums[...] = term

    @pl.when(step > 0)
    def _():
        sums[...] += term


def primal_kernel(
    place, own, plus, minus, two_x, two_g, weights, hidden, act_out, factor_out, dh_out, by_x, by_g
):
    step = pl.program_id(0)
    add_up(step, by_x, contract(pairs(place, own, plus, minus, two_x, 0), weights, 0, 2))
    add_up(step, by_g, contract(pairs(place, own, plus, minus, two_g, 1), weights, 2, 1))

    @pl.when(step == pl.num_programs(0) - 1)
    def _():
        upper = by_x[:, 320:]
        act, slope = gelu_value_slope(by_x[:, :320])
        hidden[...] = (act * upper).astype(BF16)
        act_out[...] = act
        factor_out[...] = slope * upper
        dh_out[...] = by_g[...]


def output_kernel(hidden, weights, out):
    for at in range(weights.shape[0]):
        value = jnp.dot(hidden[...], weights[at, 0], preferred_element_type=F32)
        for half in range(2):
            block = 2 * at + half
            out[block % 4, block // 4, 0] = value[:, half * 128 : (half + 1) * 128]


def tangent_kernel(
    place, own, plus, minus, two_x, two_g, weights, hidden, act, factor, dh, mask, out, by_x, by_g
):
    step = pl.program_id(0)
    add_up(step, by_x, contract(pairs(place, own, plus, minus, two_x, 0), weights, 0, 4))
    add_up(step, by_g, contract(pairs(place, own, plus, minus, two_g, 1), weights, 4, 2))

    @pl.when(step == pl.num_programs(0) - 1)
    def _():
        rows = lax.broadcasted_iota(jnp.int32, (8, 128), 0)
        lanes = lax.broadcasted_iota(jnp.int32, (8, 128), 1)
        total = jnp.zeros((8, 128), F32)
        for k in range(2):
            gate = by_x[:, k * 320 : (k + 1) * 320]
            upper = by_x[:, (2 + k) * 320 : (3 + k) * 320]
            tangent = (factor[...] * gate + act[...] * upper).astype(BF16)
            value = tangent.astype(F32) * dh[...]
            value += hidden[...].astype(F32) * by_g[:, k * 320 : (k + 1) * 320]
            value = jnp.sum(value, axis=1, keepdims=True) * mask[...]
            value = jnp.sum(value, axis=0, keepdims=True)
            total = jnp.where((rows == place[2]) & (lanes == k), value, total)
        out[...] = total


def activation_specs():
    full = pl.BlockSpec((1, 2, 2, 128, 128), lambda s, p: (s, 0, 0, 0, 0))
    single = pl.BlockSpec((1, 2, 128, 128), lambda s, p: (s, 0, 0, 0))
    return [full, full, full, single, single]


def whole(shape):
    return pl.BlockSpec(shape, lambda s, p: (0,) * len(shape))


def weight_spec(count):
    return pl.BlockSpec((2, 1, 2, count, 320, 256), lambda s, p: (0, s, 0, 0, 0, 0))


def shards(tokens, out_grad, loss_mask, w_in0, w_in1, w_out, tan_in0, tan_in1, tan_out):
    fsdp = lax.axis_index("fsdp")
    seq = lax.axis_index("seq")
    rows = tokens.shape[0]
    length = rows * lax.axis_size("seq") // EXAMPLES
    place = jnp.stack([fsdp // 16, fsdp % 4, seq * rows // length]).astype(jnp.int32)

    stack_w = jnp.stack([w_in0, w_in1, w_out])
    stack_w, *tans = lax.optimization_barrier((stack_w, tan_in0, tan_in1, tan_out))
    stack_t = jnp.concatenate(tans, axis=0)
    full_w = lax.all_gather(stack_w, "seq", axis=0).reshape(2, 4, 2, 3, 320, 256)
    full_t = lax.all_gather(stack_t, "seq", axis=0).reshape(2, 4, 2, 6, 320, 256)

    both = jnp.stack([tokens, out_grad])
    other = lax.ppermute(both, "fsdp", [(i, (i + 16) % 32) for i in range(32)])
    own = lax.all_gather(jnp.stack([both, other]), "fsdp", axis=0, axis_index_groups=Z_FAR)
    plus = z_shift(own, 1)
    minus = z_shift(own, -1)
    two_x = z_shift(own[:, :, 0], 2)
    two_g = z_shift(own[:, :, 1], -2)
    acts = (own, plus, minus, two_x, two_g)

    flat = jax.ShapeDtypeStruct((128, 320), F32)
    hidden, act, factor, dh = pl.pallas_call(
        primal_kernel,
        out_shape=(jax.ShapeDtypeStruct((128, 320), BF16), flat, flat, flat),
        grid_spec=pltpu.PrefetchScalarGridSpec(
            num_scalar_prefetch=1,
            grid=(4,),
            in_specs=activation_specs() + [weight_spec(3)],
            out_specs=(whole((128, 320)),) * 4,
            scratch_shapes=[pltpu.VMEM((128, 640), F32), pltpu.VMEM((128, 320), F32)],
        ),
        compiler_params=pltpu.CompilerParams(vmem_limit_bytes=32 * 2**20),
        cost_estimate=pl.CostEstimate(
            flops=2 * 3 * 128 * 320 * 4096, bytes_accessed=10 * 2**20, transcendentals=40960
        ),
        name="primal",
    )(place, *acts, full_w)

    partial = pl.pallas_call(
        output_kernel,
        out_shape=jax.ShapeDtypeStruct((4, 4, 2, 128, 128), F32),
        grid=(4,),
        in_specs=[
            pl.BlockSpec((128, 320), lambda s: (0, 0)),
            pl.BlockSpec((4, 1, 320, 256), lambda s: (s, 2, 0, 0)),
        ],
        out_specs=pl.BlockSpec((4, 2, 1, 128, 128), lambda s: (0, s % 2, s // 2, 0, 0)),
        compiler_params=pltpu.CompilerParams(vmem_limit_bytes=32 * 2**20),
        cost_estimate=pl.CostEstimate(
            flops=2 * 128 * 320 * 4096, bytes_accessed=5 * 2**20, transcendentals=0
        ),
        name="block_sums",
    )(hidden, full_w.reshape(16, 3, 320, 256))

    for groups in (Z_NEAR, Z_FAR, X_PAIRS):
        partial = lax.all_to_all(partial, "fsdp", 0, 0, axis_index_groups=groups)
        partial = jnp.sum(partial, axis=0)
    block_out = partial.astype(BF16)
    block_out, hidden = lax.optimization_barrier((block_out, hidden))

    terms = pl.pallas_call(
        tangent_kernel,
        out_shape=jax.ShapeDtypeStruct((8, 128), F32),
        grid_spec=pltpu.PrefetchScalarGridSpec(
            num_scalar_prefetch=1,
            grid=(4,),
            in_specs=activation_specs()
            + [weight_spec(6)]
            + [whole((128, 320))] * 4
            + [whole((128, 1))],
            out_specs=whole((8, 128)),
            scratch_shapes=[pltpu.VMEM((128, 1280), F32), pltpu.VMEM((128, 640), F32)],
        ),
        compiler_params=pltpu.CompilerParams(vmem_limit_bytes=40 * 2**20),
        cost_estimate=pl.CostEstimate(
            flops=2 * 6 * 128 * 320 * 4096, bytes_accessed=18 * 2**20, transcendentals=0
        ),
        name="tangents",
    )(place, *acts, full_t, hidden, act, factor, dh, loss_mask.astype(F32)[:, None])

    def gather_sum(value, axis, groups, size):
        copies = jnp.broadcast_to(value[None], (size,) + value.shape)
        got = lax.all_to_all(copies, axis, 0, 0, axis_index_groups=groups)
        return jnp.sum(got, axis=0)

    terms = gather_sum(terms, "fsdp", Z_ALL, 16)
    terms = gather_sum(terms, "fsdp", X_PAIRS, 2)
    terms = gather_sum(terms, "seq", None, 16)
    return (block_out, terms[:EXAMPLES, :2])


def solution(mesh):
    placed = (
        P("seq", "fsdp"),
        P("seq", "fsdp"),
        P("seq"),
        P("fsdp", "seq"),
        P("fsdp", "seq"),
        P("fsdp", "seq"),
        P(None, "fsdp", "seq"),
        P(None, "fsdp", "seq"),
        P(None, "fsdp", "seq"),
    )
    return jax.shard_map(
        shards, mesh=mesh, in_specs=placed, out_specs=(P("seq", "fsdp"), P()), check_vma=False
    )
```

```python
import functools
import math

import jax
import jax.numpy as jnp
from jax import lax
from jax.experimental import pallas as pl
from jax.experimental.pallas import tpu as pltpu
from jax.sharding import PartitionSpec as P

EXAMPLES = 4
F32 = jnp.float32
BF16 = jnp.bfloat16
NT = (((1,), (1,)), ((), ()))

Z_FAR = [[h * 16 + q * 4 + r for q in range(4)] for h in range(2) for r in range(4)]


def eights(held):
    sizes = (2, 4, 4, 4, 2, 2)
    groups = {}
    for device in range(512):
        digits, rest = [], device
        for size in reversed(sizes):
            digits.insert(0, rest % size)
            rest //= size
        groups.setdefault(tuple(digits[at] for at in held), []).append(device)
    return [groups[key] for key in sorted(groups)]


ALL_BY_EIGHT = [eights((2, 3, 4, 5)), eights((0, 1, 3, 4)), eights((0, 1, 2, 5))]


def gelu_value_slope(value):
    coeff = math.sqrt(2.0 / math.pi)
    inner = coeff * (value + 0.044715 * value * value * value)
    tangent = jnp.tanh(inner)
    act = 0.5 * value * (1.0 + tangent)
    slope = 0.5 * (1.0 + tangent) + 0.5 * value * (1.0 - tangent * tangent) * coeff * (
        1.0 + 3.0 * 0.044715 * value * value
    )
    return (act, slope)


def z_shift(array, step):
    perm = [(h * 16 + (z + step) % 16, h * 16 + z) for h in range(2) for z in range(16)]
    return lax.ppermute(array, "fsdp", perm)


def pairs(place, own, plus, minus, two, which):
    x_hi, z_lo = place[0], place[1]
    found = []
    for other in range(2):
        held = [own[0, other, which], plus[0, other, which], two[0, other], minus[0, other, which]]
        near = []
        for at in range(4):
            block = held[0]
            for shift in range(1, 4):
                block = jnp.where((z_lo + shift) % 4 == at, held[shift], block)
            near.append(block)
        row = jnp.bitwise_xor(x_hi, other)
        for half in range(2):
            block = jnp.concatenate([near[2 * half], near[2 * half + 1]], axis=1)
            found.append((row, half, block))
    return found


def contract(blocks, weights, first, count):
    total = None
    for row, half, block in blocks:
        rows = weights[row, 0, half, first : first + count].reshape(count * 320, 256)
        term = lax.dot_general(rows, block, NT, preferred_element_type=F32)
        total = term if total is None else total + term
    return total


def add_up(step, sums, term):
    @pl.when(step == 0)
    def _():
        sums[...] = term

    @pl.when(step > 0)
    def _():
        sums[...] += term


def primal_kernel(
    place, own, plus, minus, two_x, two_g, weights, hidden, across, act_out, factor_out, dh_out, by_x, by_g
):
    step = pl.program_id(0)
    add_up(step, by_x, contract(pairs(place, own, plus, minus, two_x, 0), weights, 0, 2))
    add_up(step, by_g, contract(pairs(place, own, plus, minus, two_g, 1), weights, 2, 1))

    @pl.when(step == pl.num_programs(0) - 1)
    def _():
        upper = by_x[320:]
        act, slope = gelu_value_slope(by_x[:320])
        product = act * upper
        hidden[...] = jnp.transpose(product).astype(BF16)
        across[...] = product.astype(BF16)
        act_out[...] = act
        factor_out[...] = slope * upper
        dh_out[...] = by_g[...]


def output_kernel(place, hidden, weights, own, plus, minus, two_a, two_b):
    z_lo = place[1]
    for z_hi in range(4):
        for shift in range(4):
            near = (z_lo + shift) % 4
            lanes = pl.ds(pl.multiple_of((near % 2) * 128, 128), 128)
            rows = weights[0, z_hi, near // 2, 0, :, lanes]
            value = jnp.dot(hidden[...], rows, preferred_element_type=F32)
            if shift == 0:
                own[0, z_hi] = value
            elif shift == 1:
                plus[0, z_hi] = value
            elif shift == 3:
                minus[0, z_hi] = value
            else:

                @pl.when(pl.program_id(0) == 0)
                def _():
                    two_a[z_hi] = value

                @pl.when(pl.program_id(0) == 1)
                def _():
                    two_b[z_hi] = value


def tangent_kernel(
    place, own, plus, minus, two_x, two_g, weights, across, act, factor, dh, mask, out, by_x, by_g
):
    step = pl.program_id(0)
    add_up(step, by_x, contract(pairs(place, own, plus, minus, two_x, 0), weights, 0, 4))
    add_up(step, by_g, contract(pairs(place, own, plus, minus, two_g, 1), weights, 4, 2))

    @pl.when(step == pl.num_programs(0) - 1)
    def _():
        rows = lax.broadcasted_iota(jnp.int32, (8, 128), 0)
        lanes = lax.broadcasted_iota(jnp.int32, (8, 128), 1)
        total = jnp.zeros((8, 128), F32)
        for k in range(2):
            gate = by_x[k * 320 : (k + 1) * 320]
            upper = by_x[(2 + k) * 320 : (3 + k) * 320]
            tangent = (factor[...] * gate + act[...] * upper).astype(BF16)
            value = tangent.astype(F32) * dh[...]
            value += across[...].astype(F32) * by_g[k * 320 : (k + 1) * 320]
            value = jnp.sum(value, axis=0, keepdims=True) * mask[...]
            value = jnp.sum(value, axis=1, keepdims=True)
            total = jnp.where((rows == place[2]) & (lanes == k), value, total)
        out[...] = total


def activation_specs():
    full = pl.BlockSpec((1, 2, 2, 128, 128), lambda s, p: (s, 0, 0, 0, 0))
    single = pl.BlockSpec((1, 2, 128, 128), lambda s, p: (s, 0, 0, 0))
    return [full, full, full, single, single]


def whole(shape):
    return pl.BlockSpec(shape, lambda s, p: (0,) * len(shape))


def weight_spec(count):
    return pl.BlockSpec((2, 1, 2, count, 320, 256), lambda s, p: (0, s, 0, 0, 0, 0))


def shards(tokens, out_grad, loss_mask, w_in0, w_in1, w_out, tan_in0, tan_in1, tan_out):
    fsdp = lax.axis_index("fsdp")
    seq = lax.axis_index("seq")
    rows = tokens.shape[0]
    length = rows * lax.axis_size("seq") // EXAMPLES
    place = jnp.stack([fsdp // 16, fsdp % 4, seq * rows // length]).astype(jnp.int32)

    stack_w = jnp.stack([w_in0, w_in1, w_out])
    stack_w, *tans = lax.optimization_barrier((stack_w, tan_in0, tan_in1, tan_out))
    stack_t = jnp.concatenate(tans, axis=0)
    full_w = lax.all_gather(stack_w, "seq", axis=0).reshape(2, 4, 2, 3, 320, 256)
    full_t = lax.all_gather(stack_t, "seq", axis=0).reshape(2, 4, 2, 6, 320, 256)

    both = jnp.stack([tokens, out_grad])
    other = lax.ppermute(both, "fsdp", [(i, (i + 16) % 32) for i in range(32)])
    own = lax.all_gather(jnp.stack([both, other]), "fsdp", axis=0, axis_index_groups=Z_FAR)
    plus = z_shift(own, 1)
    minus = z_shift(own, -1)
    two_x = z_shift(own[:, :, 0], 2)
    two_g = z_shift(own[:, :, 1], -2)
    acts = (own, plus, minus, two_x, two_g)

    flat = jax.ShapeDtypeStruct((320, 128), F32)
    hidden, across, act, factor, dh = pl.pallas_call(
        primal_kernel,
        out_shape=(
            jax.ShapeDtypeStruct((128, 320), BF16),
            jax.ShapeDtypeStruct((320, 128), BF16),
            flat,
            flat,
            flat,
        ),
        grid_spec=pltpu.PrefetchScalarGridSpec(
            num_scalar_prefetch=1,
            grid=(4,),
            in_specs=activation_specs() + [weight_spec(3)],
            out_specs=(whole((128, 320)),) + (whole((320, 128)),) * 4,
            scratch_shapes=[pltpu.VMEM((640, 128), F32), pltpu.VMEM((320, 128), F32)],
        ),
        compiler_params=pltpu.CompilerParams(vmem_limit_bytes=32 * 2**20),
        cost_estimate=pl.CostEstimate(
            flops=2 * 3 * 128 * 320 * 4096, bytes_accessed=10 * 2**20, transcendentals=40960
        ),
        name="primal",
    )(place, *acts, full_w)

    by_x_hi = pl.BlockSpec((1, 4, 128, 128), lambda s, p: (s, 0, 0, 0))
    half_sums = jax.ShapeDtypeStruct((4, 128, 128), F32)
    both_sums = jax.ShapeDtypeStruct((2, 4, 128, 128), F32)
    kept, up, down, two_up, two_down = pl.pallas_call(
        output_kernel,
        out_shape=(both_sums, both_sums, both_sums, half_sums, half_sums),
        grid_spec=pltpu.PrefetchScalarGridSpec(
            num_scalar_prefetch=1,
            grid=(2,),
            in_specs=[
                whole((128, 320)),
                pl.BlockSpec(
                    (1, 4, 2, 1, 320, 256),
                    lambda s, p: (jnp.bitwise_xor(p[0], s), 0, 0, 2, 0, 0),
                ),
            ],
            out_specs=(by_x_hi, by_x_hi, by_x_hi, whole((4, 128, 128)), whole((4, 128, 128))),
        ),
        compiler_params=pltpu.CompilerParams(vmem_limit_bytes=32 * 2**20),
        cost_estimate=pl.CostEstimate(
            flops=2 * 128 * 320 * 4096, bytes_accessed=5 * 2**20, transcendentals=0
        ),
        name="block_sums",
    )(place, hidden, full_w)

    up = z_shift(up, -1)
    down = z_shift(down, 1)
    two_up = z_shift(two_up, -2)
    two_down = z_shift(two_down, 2)
    away = kept[1] + up[1] + down[1] + two_down
    away = lax.ppermute(away, "fsdp", [(i, (i + 16) % 32) for i in range(32)])
    partial = kept[0] + up[0] + down[0] + two_up + away
    partial = jnp.sum(lax.all_to_all(partial, "fsdp", 0, 0, axis_index_groups=Z_FAR), axis=0)
    block_out = partial.astype(BF16)
    block_out, across = lax.optimization_barrier((block_out, across))

    terms = pl.pallas_call(
        tangent_kernel,
        out_shape=jax.ShapeDtypeStruct((8, 128), F32),
        grid_spec=pltpu.PrefetchScalarGridSpec(
            num_scalar_prefetch=1,
            grid=(4,),
            in_specs=activation_specs()
            + [weight_spec(6)]
            + [whole((320, 128))] * 4
            + [whole((1, 128))],
            out_specs=whole((8, 128)),
            scratch_shapes=[pltpu.VMEM((1280, 128), F32), pltpu.VMEM((640, 128), F32)],
        ),
        compiler_params=pltpu.CompilerParams(vmem_limit_bytes=40 * 2**20),
        cost_estimate=pl.CostEstimate(
            flops=2 * 6 * 128 * 320 * 4096, bytes_accessed=18 * 2**20, transcendentals=0
        ),
        name="tangents",
    )(place, *acts, full_t, across, act, factor, dh, loss_mask.astype(F32)[None])

    for groups in ALL_BY_EIGHT:
        copies = jnp.broadcast_to(terms[None], (8,) + terms.shape)
        got = lax.all_to_all(copies, ("fsdp", "seq"), 0, 0, axis_index_groups=groups)
        terms = jnp.sum(got, axis=0)
    return (block_out, terms[:EXAMPLES, :2])


def solution(mesh):
    placed = (
        P("seq", "fsdp"),
        P("seq", "fsdp"),
        P("seq"),
        P("fsdp", "seq"),
        P("fsdp", "seq"),
        P("fsdp", "seq"),
        P(None, "fsdp", "seq"),
        P(None, "fsdp", "seq"),
        P(None, "fsdp", "seq"),
    )
    return jax.shard_map(
        shards, mesh=mesh, in_specs=placed, out_specs=(P("seq", "fsdp"), P()), check_vma=False
    )
```

```python
import functools
import math

import jax
import jax.numpy as jnp
from jax import lax
from jax.experimental import pallas as pl
from jax.experimental.pallas import tpu as pltpu
from jax.sharding import PartitionSpec as P

EXAMPLES = 4
F32 = jnp.float32
BF16 = jnp.bfloat16
NT = (((1,), (1,)), ((), ()))

Z_FAR = [[h * 16 + q * 4 + r for q in range(4)] for h in range(2) for r in range(4)]
Z_ALL = [list(range(16)), list(range(16, 32))]
X_PAIRS = [[i, i + 16] for i in range(16)]


def gelu_value_slope(value):
    coeff = math.sqrt(2.0 / math.pi)
    inner = coeff * (value + 0.044715 * value * value * value)
    tangent = jnp.tanh(inner)
    act = 0.5 * value * (1.0 + tangent)
    slope = 0.5 * (1.0 + tangent) + 0.5 * value * (1.0 - tangent * tangent) * coeff * (
        1.0 + 3.0 * 0.044715 * value * value
    )
    return (act, slope)


def z_shift(array, step):
    perm = [(h * 16 + (z + step) % 16, h * 16 + z) for h in range(2) for z in range(16)]
    return lax.ppermute(array, "fsdp", perm)


def y_shift(array, step):
    return lax.ppermute(array, "seq", [((i + 4 * step) % 16, i) for i in range(16)])


def pairs(place, own, plus, minus, two, which):
    x_hi, z_lo = place[0], place[1]
    found = []
    for other in range(2):
        held = [own[0, other, which], plus[0, other, which], two[0, other], minus[0, other, which]]
        near = []
        for at in range(4):
            block = held[0]
            for shift in range(1, 4):
                block = jnp.where((z_lo + shift) % 4 == at, held[shift], block)
            near.append(block)
        row = jnp.bitwise_xor(x_hi, other)
        for half in range(2):
            block = jnp.concatenate([near[2 * half], near[2 * half + 1]], axis=1)
            found.append((row, half, block))
    return found


def contract(blocks, weights, first, count):
    total = None
    for row, half, block in blocks:
        rows = weights[row, 0, half, first : first + count].reshape(count * 320, 256)
        term = lax.dot_general(rows, block, NT, preferred_element_type=F32)
        total = term if total is None else total + term
    return total


def add_up(step, sums, term):
    @pl.when(step == 0)
    def _():
        sums[...] = term

    @pl.when(step > 0)
    def _():
        sums[...] += term


def primal_kernel(
    place, own, plus, minus, two_x, two_g, weights, hidden, across, act_out, factor_out, dh_out, by_x, by_g
):
    step = pl.program_id(0)
    add_up(step, by_x, contract(pairs(place, own, plus, minus, two_x, 0), weights, 0, 2))
    add_up(step, by_g, contract(pairs(place, own, plus, minus, two_g, 1), weights, 2, 1))

    @pl.when(step == pl.num_programs(0) - 1)
    def _():
        upper = by_x[320:]
        act, slope = gelu_value_slope(by_x[:320])
        product = act * upper
        hidden[...] = jnp.transpose(product).astype(BF16)
        across[...] = product.astype(BF16)
        act_out[...] = act
        factor_out[...] = slope * upper
        dh_out[...] = by_g[...]


def output_kernel(place, hidden, weights, own, plus, minus, two_a, two_b):
    z_lo = place[1]
    for z_hi in range(4):
        for shift in range(4):
            near = (z_lo + shift) % 4
            lanes = pl.ds(pl.multiple_of((near % 2) * 128, 128), 128)
            rows = weights[0, z_hi, near // 2, 0, :, lanes]
            value = jnp.dot(hidden[...], rows, preferred_element_type=F32)
            if shift == 0:
                own[0, z_hi] = value
            elif shift == 1:
                plus[0, z_hi] = value
            elif shift == 3:
                minus[0, z_hi] = value
            else:

                @pl.when(pl.program_id(0) == 0)
                def _():
                    two_a[z_hi] = value

                @pl.when(pl.program_id(0) == 1)
                def _():
                    two_b[z_hi] = value


def by_core(place, blocks, same):
    first = (place[5] == 0) if same else (place[5] == 1)
    at = {}
    for index, (_, half, block) in enumerate(blocks):
        at[index // 2, half] = block
    return [jnp.where(first, at[index, 0], at[index, 1]) for index in range(2)]


def contract_moved(place, blocks, mine, theirs, first, count):
    total = None
    for refs, same in ((mine, True), (theirs, False)):
        for ref, block in zip(refs, by_core(place, blocks, same)):
            rows = ref[0, 0, first : first + count].reshape(count * 320, 256)
            term = lax.dot_general(rows, block, NT, preferred_element_type=F32)
            total = term if total is None else total + term
    return total


def tangent_kernel(
    place,
    own,
    plus,
    minus,
    two_x,
    two_g,
    weights,
    mine_0,
    mine_1,
    theirs_0,
    theirs_1,
    across,
    act,
    factor,
    dh,
    mask,
    out,
    by_x,
    by_g,
):
    step = pl.program_id(0)
    of_x = pairs(place, own, plus, minus, two_x, 0)
    of_g = pairs(place, own, plus, minus, two_g, 1)
    moved = ((mine_0, mine_1), (theirs_0, theirs_1))
    add_up(step, by_x.at[:960], contract(of_x, weights, 0, 3))
    add_up(step, by_x.at[960:], contract_moved(place, of_x, *moved, 0, 1))
    add_up(step, by_g, contract_moved(place, of_g, *moved, 1, 2))

    @pl.when(step == pl.num_programs(0) - 1)
    def _():
        rows = lax.broadcasted_iota(jnp.int32, (8, 128), 0)
        lanes = lax.broadcasted_iota(jnp.int32, (8, 128), 1)
        total = jnp.zeros((8, 128), F32)
        for k in range(2):
            gate = by_x[k * 320 : (k + 1) * 320]
            upper = by_x[(2 + k) * 320 : (3 + k) * 320]
            tangent = (factor[...] * gate + act[...] * upper).astype(BF16)
            value = tangent.astype(F32) * dh[...]
            value += across[...].astype(F32) * by_g[k * 320 : (k + 1) * 320]
            value = jnp.sum(value, axis=0, keepdims=True) * mask[...]
            value = jnp.sum(value, axis=1, keepdims=True)
            total = jnp.where((rows == place[2]) & (lanes == k), value, total)
        out[...] = total


def activation_specs():
    full = pl.BlockSpec((1, 2, 2, 128, 128), lambda s, p: (s, 0, 0, 0, 0))
    single = pl.BlockSpec((1, 2, 128, 128), lambda s, p: (s, 0, 0, 0))
    return [full, full, full, single, single]


def whole(shape):
    return pl.BlockSpec(shape, lambda s, p: (0,) * len(shape))


def weight_spec(count):
    return pl.BlockSpec((2, 1, 2, count, 320, 256), lambda s, p: (0, s, 0, 0, 0, 0))


def moved_spec(other):
    def index(s, p):
        y = jnp.bitwise_xor(p[0], other) * 2 + s // 2
        return ((y - p[3] + 4) % 4, jnp.bitwise_xor(s % 2, p[4]), 0, 0, 0)

    return pl.BlockSpec((1, 1, 3, 320, 256), index)


def shards(tokens, out_grad, loss_mask, w_in0, w_in1, w_out, tan_in0, tan_in1, tan_out):
    fsdp = lax.axis_index("fsdp")
    seq = lax.axis_index("seq")
    rows = tokens.shape[0]
    length = rows * lax.axis_size("seq") // EXAMPLES
    place = jnp.stack(
        [fsdp // 16, fsdp % 4, seq * rows // length, seq // 4, seq // 2 % 2, seq % 2]
    ).astype(jnp.int32)

    stack_w = jnp.stack([w_in0, w_in1, w_out])
    both = jnp.stack([tokens, out_grad])
    _, _, tan_in0, tan_in1, tan_out = lax.optimization_barrier(
        (stack_w, both, tan_in0, tan_in1, tan_out)
    )
    stack_t = jnp.concatenate([tan_in0, tan_in1[:1]], axis=0)
    moved = jnp.concatenate([tan_in1[1:], tan_out], axis=0)
    full_w = lax.all_gather(stack_w, "seq", axis=0).reshape(2, 4, 2, 3, 320, 256)
    full_t = lax.all_gather(stack_t, "seq", axis=0).reshape(2, 4, 2, 3, 320, 256)

    other = lax.ppermute(both, "fsdp", [(i, (i + 16) % 32) for i in range(32)])
    own = lax.all_gather(jnp.stack([both, other]), "fsdp", axis=0, axis_index_groups=Z_FAR)
    plus = z_shift(own, 1)
    minus = z_shift(own, -1)
    two_x = z_shift(own[:, :, 0], 2)
    two_g = z_shift(own[:, :, 1], -2)
    acts = (own, plus, minus, two_x, two_g)

    moved_x = lax.ppermute(moved, "seq", [(i, i ^ 2) for i in range(16)])
    moved, *_ = lax.optimization_barrier((moved,) + acts)
    moved = jnp.stack([moved, moved_x])
    moved_plus, moved_minus = y_shift(moved, 1), y_shift(moved, -1)

    flat = jax.ShapeDtypeStruct((320, 128), F32)
    hidden, across, act, factor, dh = pl.pallas_call(
        primal_kernel,
        out_shape=(
            jax.ShapeDtypeStruct((128, 320), BF16),
            jax.ShapeDtypeStruct((320, 128), BF16),
            flat,
            flat,
            flat,
        ),
        grid_spec=pltpu.PrefetchScalarGridSpec(
            num_scalar_prefetch=1,
            grid=(4,),
            in_specs=activation_specs() + [weight_spec(3)],
            out_specs=(whole((128, 320)),) + (whole((320, 128)),) * 4,
            scratch_shapes=[pltpu.VMEM((640, 128), F32), pltpu.VMEM((320, 128), F32)],
        ),
        compiler_params=pltpu.CompilerParams(vmem_limit_bytes=32 * 2**20),
        cost_estimate=pl.CostEstimate(
            flops=2 * 3 * 128 * 320 * 4096, bytes_accessed=10 * 2**20, transcendentals=40960
        ),
        name="primal",
    )(place, *acts, full_w)

    by_x_hi = pl.BlockSpec((1, 4, 128, 128), lambda s, p: (s, 0, 0, 0))
    half_sums = jax.ShapeDtypeStruct((4, 128, 128), F32)
    both_sums = jax.ShapeDtypeStruct((2, 4, 128, 128), F32)
    kept, up, down, two_up, two_down = pl.pallas_call(
        output_kernel,
        out_shape=(both_sums, both_sums, both_sums, half_sums, half_sums),
        grid_spec=pltpu.PrefetchScalarGridSpec(
            num_scalar_prefetch=1,
            grid=(2,),
            in_specs=[
                whole((128, 320)),
                pl.BlockSpec(
                    (1, 4, 2, 1, 320, 256),
                    lambda s, p: (jnp.bitwise_xor(p[0], s), 0, 0, 2, 0, 0),
                ),
            ],
            out_specs=(by_x_hi, by_x_hi, by_x_hi, whole((4, 128, 128)), whole((4, 128, 128))),
        ),
        compiler_params=pltpu.CompilerParams(vmem_limit_bytes=32 * 2**20),
        cost_estimate=pl.CostEstimate(
            flops=2 * 128 * 320 * 4096, bytes_accessed=5 * 2**20, transcendentals=0
        ),
        name="block_sums",
    )(place, hidden, full_w)

    half_plus, half_minus, _ = lax.optimization_barrier((moved_plus[0], moved_minus[1], kept))
    half_plus, half_minus = y_shift(half_plus, 1), y_shift(half_minus, -1)

    up = z_shift(up, -1)
    down = z_shift(down, 1)
    two_up = z_shift(two_up, -2)
    two_down = z_shift(two_down, 2)
    away = kept[1] + up[1] + down[1] + two_down
    across, half_plus, half_minus, _ = lax.optimization_barrier(
        (across, half_plus, half_minus, away)
    )
    mine = jnp.stack([moved, moved_plus, jnp.stack([half_plus, half_minus]), moved_minus])
    theirs = lax.ppermute(mine, "seq", [(i, i ^ 1) for i in range(16)])
    away = lax.ppermute(away, "fsdp", [(i, (i + 16) % 32) for i in range(32)])
    partial = kept[0] + up[0] + down[0] + two_up + away

    terms = pl.pallas_call(
        tangent_kernel,
        out_shape=jax.ShapeDtypeStruct((8, 128), F32),
        grid_spec=pltpu.PrefetchScalarGridSpec(
            num_scalar_prefetch=1,
            grid=(4,),
            in_specs=activation_specs()
            + [weight_spec(3), moved_spec(0), moved_spec(1), moved_spec(0), moved_spec(1)]
            + [whole((320, 128))] * 4
            + [whole((1, 128))],
            out_specs=whole((8, 128)),
            scratch_shapes=[pltpu.VMEM((1280, 128), F32), pltpu.VMEM((640, 128), F32)],
        ),
        compiler_params=pltpu.CompilerParams(vmem_limit_bytes=40 * 2**20),
        cost_estimate=pl.CostEstimate(
            flops=2 * 6 * 128 * 320 * 4096, bytes_accessed=18 * 2**20, transcendentals=0
        ),
        name="tangents",
    )(place, *acts, full_t, mine, mine, theirs, theirs, across, act, factor, dh, loss_mask.astype(F32)[None])

    partial, _ = lax.optimization_barrier((partial, terms))
    z_hi = fsdp // 4 % 4
    total = lax.dynamic_index_in_dim(partial, z_hi, 0, False)
    far = [
        z_shift(lax.dynamic_index_in_dim(partial, (z_hi + 4 - step) % 4, 0, False), 4 * step)
        for step in range(1, 4)
    ]

    for axis, size, groups in (("seq", 16, None), ("fsdp", 16, Z_ALL), ("fsdp", 2, X_PAIRS)):
        copies = jnp.broadcast_to(terms[None], (size,) + terms.shape)
        terms = jnp.sum(lax.all_to_all(copies, axis, 0, 0, axis_index_groups=groups), axis=0)
    block_out = (total + far[0] + far[1] + far[2]).astype(BF16)
    return (block_out, terms[:EXAMPLES, :2])


def solution(mesh):
    placed = (
        P("seq", "fsdp"),
        P("seq", "fsdp"),
        P("seq"),
        P("fsdp", "seq"),
        P("fsdp", "seq"),
        P("fsdp", "seq"),
        P(None, "fsdp", "seq"),
        P(None, "fsdp", "seq"),
        P(None, "fsdp", "seq"),
    )
    return jax.shard_map(
        shards, mesh=mesh, in_specs=placed, out_specs=(P("seq", "fsdp"), P()), check_vma=False
    )
```

```python
import functools
import math

import jax
import jax.numpy as jnp
from jax import lax
from jax.experimental import pallas as pl
from jax.experimental.pallas import tpu as pltpu
from jax.sharding import PartitionSpec as P

EXAMPLES = 4
F32 = jnp.float32
BF16 = jnp.bfloat16
NT = (((1,), (1,)), ((), ()))

Z_FAR = [[h * 16 + q * 4 + r for q in range(4)] for h in range(2) for r in range(4)]
Z_ALL = [list(range(16)), list(range(16, 32))]
X_PAIRS = [[i, i + 16] for i in range(16)]


def gelu_value_slope(value):
    coeff = math.sqrt(2.0 / math.pi)
    inner = coeff * (value + 0.044715 * value * value * value)
    tangent = jnp.tanh(inner)
    act = 0.5 * value * (1.0 + tangent)
    slope = 0.5 * (1.0 + tangent) + 0.5 * value * (1.0 - tangent * tangent) * coeff * (
        1.0 + 3.0 * 0.044715 * value * value
    )
    return (act, slope)


def z_shift(array, step):
    perm = [(h * 16 + (z + step) % 16, h * 16 + z) for h in range(2) for z in range(16)]
    return lax.ppermute(array, "fsdp", perm)


def y_shift(array, step):
    return lax.ppermute(array, "seq", [((i + 4 * step) % 16, i) for i in range(16)])


def pairs(place, own, plus, minus, two, which):
    x_hi, z_lo = place[0], place[1]
    found = []
    for other in range(2):
        held = [own[0, other, which], plus[0, other, which], two[0, other], minus[0, other, which]]
        near = []
        for at in range(4):
            block = held[0]
            for shift in range(1, 4):
                block = jnp.where((z_lo + shift) % 4 == at, held[shift], block)
            near.append(block)
        row = jnp.bitwise_xor(x_hi, other)
        for half in range(2):
            block = jnp.concatenate([near[2 * half], near[2 * half + 1]], axis=1)
            found.append((row, half, block))
    return found


def contract(blocks, weights, first, count):
    total = None
    for row, half, block in blocks:
        rows = weights[row, 0, half, first : first + count].reshape(count * 320, 256)
        term = lax.dot_general(rows, block, NT, preferred_element_type=F32)
        total = term if total is None else total + term
    return total


def add_up(step, sums, term):
    @pl.when(step == 0)
    def _():
        sums[...] = term

    @pl.when(step > 0)
    def _():
        sums[...] += term


def primal_kernel(
    place, own, plus, minus, two_x, two_g, weights, hidden, across, act_out, factor_out, dh_out, by_x, by_g
):
    step = pl.program_id(0)
    add_up(step, by_x, contract(pairs(place, own, plus, minus, two_x, 0), weights, 0, 2))
    add_up(step, by_g, contract(pairs(place, own, plus, minus, two_g, 1), weights, 2, 1))

    @pl.when(step == pl.num_programs(0) - 1)
    def _():
        upper = by_x[320:]
        act, slope = gelu_value_slope(by_x[:320])
        product = act * upper
        hidden[...] = jnp.transpose(product).astype(BF16)
        across[...] = product.astype(BF16)
        act_out[...] = act
        factor_out[...] = slope * upper
        dh_out[...] = by_g[...]


def output_kernel(place, hidden, weights, own, plus, minus, two_a, two_b):
    z_lo = place[1]
    for z_hi in range(4):
        for shift in range(4):
            near = (z_lo + shift) % 4
            lanes = pl.ds(pl.multiple_of((near % 2) * 128, 128), 128)
            rows = weights[0, z_hi, near // 2, 0, :, lanes]
            value = jnp.dot(hidden[...], rows, preferred_element_type=F32)
            if shift == 0:
                own[0, z_hi] = value
            elif shift == 1:
                plus[0, z_hi] = value
            elif shift == 3:
                minus[0, z_hi] = value
            else:

                @pl.when(pl.program_id(0) == 0)
                def _():
                    two_a[z_hi] = value

                @pl.when(pl.program_id(0) == 1)
                def _():
                    two_b[z_hi] = value


def by_core(place, blocks, same):
    first = (place[5] == 0) if same else (place[5] == 1)
    at = {}
    for index, (_, half, block) in enumerate(blocks):
        at[index // 2, half] = block
    return [jnp.where(first, at[index, 0], at[index, 1]) for index in range(2)]


def contract_moved(place, blocks, mine, theirs, first, count):
    total = None
    for refs, same in ((mine, True), (theirs, False)):
        for ref, block in zip(refs, by_core(place, blocks, same)):
            rows = ref[0, 0, first : first + count].reshape(count * 320, 256)
            term = lax.dot_general(rows, block, NT, preferred_element_type=F32)
            total = term if total is None else total + term
    return total


def tangent_kernel(
    place,
    own,
    plus,
    minus,
    two_x,
    two_g,
    weights,
    mine_0,
    mine_1,
    theirs_0,
    theirs_1,
    across,
    act,
    factor,
    dh,
    mask,
    out,
    by_x,
    by_g,
):
    step = pl.program_id(0)
    of_x = pairs(place, own, plus, minus, two_x, 0)
    of_g = pairs(place, own, plus, minus, two_g, 1)
    moved = ((mine_0, mine_1), (theirs_0, theirs_1))
    add_up(step, by_x.at[:960], contract(of_x, weights, 0, 3))
    add_up(step, by_x.at[960:], contract_moved(place, of_x, *moved, 0, 1))
    add_up(step, by_g, contract_moved(place, of_g, *moved, 1, 2))

    @pl.when(step == pl.num_programs(0) - 1)
    def _():
        rows = lax.broadcasted_iota(jnp.int32, (8, 128), 0)
        lanes = lax.broadcasted_iota(jnp.int32, (8, 128), 1)
        total = jnp.zeros((8, 128), F32)
        for k in range(2):
            gate = by_x[k * 320 : (k + 1) * 320]
            upper = by_x[(2 + k) * 320 : (3 + k) * 320]
            tangent = (factor[...] * gate + act[...] * upper).astype(BF16)
            value = tangent.astype(F32) * dh[...]
            value += across[...].astype(F32) * by_g[k * 320 : (k + 1) * 320]
            value = jnp.sum(value, axis=0, keepdims=True) * mask[...]
            value = jnp.sum(value, axis=1, keepdims=True)
            total = jnp.where((rows == place[2]) & (lanes == k), value, total)
        out[...] = total


def activation_specs():
    full = pl.BlockSpec((1, 2, 2, 128, 128), lambda s, p: (s, 0, 0, 0, 0))
    single = pl.BlockSpec((1, 2, 128, 128), lambda s, p: (s, 0, 0, 0))
    return [full, full, full, single, single]


def whole(shape):
    return pl.BlockSpec(shape, lambda s, p: (0,) * len(shape))


def weight_spec(count):
    return pl.BlockSpec((2, 1, 2, count, 320, 256), lambda s, p: (0, s, 0, 0, 0, 0))


def moved_spec(other):
    def index(s, p):
        y = jnp.bitwise_xor(p[0], other) * 2 + s // 2
        return ((y - p[3] + 4) % 4, jnp.bitwise_xor(s % 2, p[4]), 0, 0, 0)

    return pl.BlockSpec((1, 1, 3, 320, 256), index)


def shards(tokens, out_grad, loss_mask, w_in0, w_in1, w_out, tan_in0, tan_in1, tan_out):
    fsdp = lax.axis_index("fsdp")
    seq = lax.axis_index("seq")
    rows = tokens.shape[0]
    length = rows * lax.axis_size("seq") // EXAMPLES
    place = jnp.stack(
        [fsdp // 16, fsdp % 4, seq * rows // length, seq // 4, seq // 2 % 2, seq % 2]
    ).astype(jnp.int32)

    stack_w = jnp.stack([w_in0, w_in1, w_out])
    both = jnp.stack([tokens, out_grad])
    _, _, tan_in0, tan_in1, tan_out = lax.optimization_barrier(
        (stack_w, both, tan_in0, tan_in1, tan_out)
    )
    stack_t = jnp.concatenate([tan_in0, tan_in1[:1]], axis=0)
    moved = jnp.concatenate([tan_in1[1:], tan_out], axis=0)
    full_w = lax.all_gather(stack_w, "seq", axis=0).reshape(2, 4, 2, 3, 320, 256)
    full_t = lax.all_gather(stack_t, "seq", axis=0).reshape(2, 4, 2, 3, 320, 256)

    other = lax.ppermute(both, "fsdp", [(i, (i + 16) % 32) for i in range(32)])
    moved_x = lax.ppermute(moved, "seq", [(i, i ^ 2) for i in range(16)])
    both, other, moved, moved_x = lax.optimization_barrier((both, other, moved, moved_x))
    own = lax.all_gather(jnp.stack([both, other]), "fsdp", axis=0, axis_index_groups=Z_FAR)
    plus = z_shift(own, 1)
    minus = z_shift(own, -1)
    two_x = z_shift(own[:, :, 0], 2)
    two_g = z_shift(own[:, :, 1], -2)
    acts = (own, plus, minus, two_x, two_g)

    moved = jnp.stack([moved, moved_x])
    moved, _ = lax.optimization_barrier((moved, own))
    moved_plus = y_shift(moved, 1)
    behind, half_plus, *_ = lax.optimization_barrier((moved, moved_plus[0]) + acts)
    moved_minus = y_shift(behind, -1)
    half_plus = y_shift(half_plus, 1)

    flat = jax.ShapeDtypeStruct((320, 128), F32)
    hidden, across, act, factor, dh = pl.pallas_call(
        primal_kernel,
        out_shape=(
            jax.ShapeDtypeStruct((128, 320), BF16),
            jax.ShapeDtypeStruct((320, 128), BF16),
            flat,
            flat,
            flat,
        ),
        grid_spec=pltpu.PrefetchScalarGridSpec(
            num_scalar_prefetch=1,
            grid=(4,),
            in_specs=activation_specs() + [weight_spec(3)],
            out_specs=(whole((128, 320)),) + (whole((320, 128)),) * 4,
            scratch_shapes=[pltpu.VMEM((640, 128), F32), pltpu.VMEM((320, 128), F32)],
        ),
        compiler_params=pltpu.CompilerParams(vmem_limit_bytes=32 * 2**20),
        cost_estimate=pl.CostEstimate(
            flops=2 * 3 * 128 * 320 * 4096, bytes_accessed=10 * 2**20, transcendentals=40960
        ),
        name="primal",
    )(place, *acts, full_w)

    by_x_hi = pl.BlockSpec((1, 4, 128, 128), lambda s, p: (s, 0, 0, 0))
    half_sums = jax.ShapeDtypeStruct((4, 128, 128), F32)
    both_sums = jax.ShapeDtypeStruct((2, 4, 128, 128), F32)
    kept, up, down, two_up, two_down = pl.pallas_call(
        output_kernel,
        out_shape=(both_sums, both_sums, both_sums, half_sums, half_sums),
        grid_spec=pltpu.PrefetchScalarGridSpec(
            num_scalar_prefetch=1,
            grid=(2,),
            in_specs=[
                whole((128, 320)),
                pl.BlockSpec(
                    (1, 4, 2, 1, 320, 256),
                    lambda s, p: (jnp.bitwise_xor(p[0], s), 0, 0, 2, 0, 0),
                ),
            ],
            out_specs=(by_x_hi, by_x_hi, by_x_hi, whole((4, 128, 128)), whole((4, 128, 128))),
        ),
        compiler_params=pltpu.CompilerParams(vmem_limit_bytes=32 * 2**20),
        cost_estimate=pl.CostEstimate(
            flops=2 * 128 * 320 * 4096, bytes_accessed=5 * 2**20, transcendentals=0
        ),
        name="block_sums",
    )(place, hidden, full_w)

    half_minus, _ = lax.optimization_barrier((moved_minus[1], kept))
    half_minus = y_shift(half_minus, -1)

    up = z_shift(up, -1)
    down = z_shift(down, 1)
    two_up = z_shift(two_up, -2)
    two_down = z_shift(two_down, 2)
    away = kept[1] + up[1] + down[1] + two_down
    across, half_plus, half_minus, _ = lax.optimization_barrier(
        (across, half_plus, half_minus, away)
    )
    mine = jnp.stack([moved, moved_plus, jnp.stack([half_plus, half_minus]), moved_minus])
    theirs = lax.ppermute(mine, "seq", [(i, i ^ 1) for i in range(16)])
    away = lax.ppermute(away, "fsdp", [(i, (i + 16) % 32) for i in range(32)])
    partial = kept[0] + up[0] + down[0] + two_up + away
    partial = jnp.sum(lax.all_to_all(partial, "fsdp", 0, 0, axis_index_groups=Z_FAR), axis=0)
    block_out = partial.astype(BF16)

    terms = pl.pallas_call(
        tangent_kernel,
        out_shape=jax.ShapeDtypeStruct((8, 128), F32),
        grid_spec=pltpu.PrefetchScalarGridSpec(
            num_scalar_prefetch=1,
            grid=(4,),
            in_specs=activation_specs()
            + [weight_spec(3), moved_spec(0), moved_spec(1), moved_spec(0), moved_spec(1)]
            + [whole((320, 128))] * 4
            + [whole((1, 128))],
            out_specs=whole((8, 128)),
            scratch_shapes=[pltpu.VMEM((1280, 128), F32), pltpu.VMEM((640, 128), F32)],
        ),
        compiler_params=pltpu.CompilerParams(vmem_limit_bytes=40 * 2**20),
        cost_estimate=pl.CostEstimate(
            flops=2 * 6 * 128 * 320 * 4096, bytes_accessed=18 * 2**20, transcendentals=0
        ),
        name="tangents",
    )(place, *acts, full_t, mine, mine, theirs, theirs, across, act, factor, dh, loss_mask.astype(F32)[None])

    for axis, size, groups in (("seq", 16, None), ("fsdp", 16, Z_ALL), ("fsdp", 2, X_PAIRS)):
        copies = jnp.broadcast_to(terms[None], (size,) + terms.shape)
        terms = jnp.sum(lax.all_to_all(copies, axis, 0, 0, axis_index_groups=groups), axis=0)
    return (block_out, terms[:EXAMPLES, :2])


def solution(mesh):
    placed = (
        P("seq", "fsdp"),
        P("seq", "fsdp"),
        P("seq"),
        P("fsdp", "seq"),
        P("fsdp", "seq"),
        P("fsdp", "seq"),
        P(None, "fsdp", "seq"),
        P(None, "fsdp", "seq"),
        P(None, "fsdp", "seq"),
    )
    return jax.shard_map(
        shards, mesh=mesh, in_specs=placed, out_specs=(P("seq", "fsdp"), P()), check_vma=False
    )
```

```python
import functools
import math

import jax
import jax.numpy as jnp
from jax import lax
from jax.experimental import pallas as pl
from jax.experimental.pallas import tpu as pltpu
from jax.sharding import PartitionSpec as P

EXAMPLES = 4
F32 = jnp.float32
BF16 = jnp.bfloat16
NT = (((1,), (1,)), ((), ()))

Z_FAR = [[h * 16 + q * 4 + r for q in range(4)] for h in range(2) for r in range(4)]
Z_ALL = [list(range(16)), list(range(16, 32))]
X_PAIRS = [[i, i + 16] for i in range(16)]


def gelu_value_slope(value):
    coeff = math.sqrt(2.0 / math.pi)
    inner = coeff * (value + 0.044715 * value * value * value)
    tangent = jnp.tanh(inner)
    act = 0.5 * value * (1.0 + tangent)
    slope = 0.5 * (1.0 + tangent) + 0.5 * value * (1.0 - tangent * tangent) * coeff * (
        1.0 + 3.0 * 0.044715 * value * value
    )
    return (act, slope)


def z_shift(array, step):
    perm = [(h * 16 + (z + step) % 16, h * 16 + z) for h in range(2) for z in range(16)]
    return lax.ppermute(array, "fsdp", perm)


def y_shift(array, step):
    return lax.ppermute(array, "seq", [((i + 4 * step) % 16, i) for i in range(16)])


def pairs(place, acts, which):
    x_hi, z_lo = place[0], place[1]
    found = []
    for other in range(2):
        near = []
        for at in range(4):
            block = acts[0, other, which, 0]
            for shift in range(1, 4):
                block = jnp.where((z_lo + shift) % 4 == at, acts[0, other, which, shift], block)
            near.append(block)
        row = jnp.bitwise_xor(x_hi, other)
        for half in range(2):
            block = jnp.concatenate([near[2 * half], near[2 * half + 1]], axis=1)
            found.append((row, half, block))
    return found


def contract(blocks, weights, first, count):
    total = None
    for row, half, block in blocks:
        rows = weights[row, 0, half, first : first + count].reshape(count * 320, 256)
        term = lax.dot_general(rows, block, NT, preferred_element_type=F32)
        total = term if total is None else total + term
    return total


def add_up(step, sums, term):
    @pl.when(step == 0)
    def _():
        sums[...] = term

    @pl.when(step > 0)
    def _():
        sums[...] += term


def primal_kernel(
    place, acts, weights, hidden, across, act_out, factor_out, dh_out, by_x, by_g
):
    step = pl.program_id(0)
    add_up(step, by_x, contract(pairs(place, acts, 0), weights, 0, 2))
    add_up(step, by_g, contract(pairs(place, acts, 1), weights, 2, 1))

    @pl.when(step == pl.num_programs(0) - 1)
    def _():
        upper = by_x[320:]
        act, slope = gelu_value_slope(by_x[:320])
        product = act * upper
        hidden[...] = jnp.transpose(product).astype(BF16)
        across[...] = product.astype(BF16)
        act_out[...] = act
        factor_out[...] = slope * upper
        dh_out[...] = by_g[...]


def output_kernel(place, hidden, weights, own, plus, minus, two_a, two_b):
    z_lo = place[1]
    for z_hi in range(4):
        for shift in range(4):
            near = (z_lo + shift) % 4
            lanes = pl.ds(pl.multiple_of((near % 2) * 128, 128), 128)
            rows = weights[0, z_hi, near // 2, 0, :, lanes]
            value = jnp.dot(hidden[...], rows, preferred_element_type=F32)
            if shift == 0:
                own[0, z_hi] = value
            elif shift == 1:
                plus[0, z_hi] = value
            elif shift == 3:
                minus[0, z_hi] = value
            else:

                @pl.when(pl.program_id(0) == 0)
                def _():
                    two_a[z_hi] = value

                @pl.when(pl.program_id(0) == 1)
                def _():
                    two_b[z_hi] = value


def column_blocks(place, acts, partner, which):
    own = pairs(place, acts, which)
    theirs = pairs(place, partner, which)
    both = [jnp.concatenate([a[2], b[2]], axis=0) for a, b in zip(own, theirs)]
    found = []
    for other in range(2):
        low, high = both[2 * other], both[2 * other + 1]
        found.append(jnp.where(place[5] == 0, low, high))
        found.append(jnp.where(place[5] == 0, high, low))
    return found


def column_sums(blocks, rows, first, count):
    total = None
    for ref, block in zip(rows, blocks):
        part = ref[0, first : first + count].reshape(count * 320, 256)
        term = lax.dot_general(part, block, NT, preferred_element_type=F32)
        total = term if total is None else total + term
    return total


def column_kernel(
    place, acts, partner, mine_0, theirs_0, mine_1, theirs_1, kept, away, by_x, by_g
):
    step = pl.program_id(0)
    rows = (mine_0, theirs_0, mine_1, theirs_1)
    add_up(step, by_x, column_sums(column_blocks(place, acts, partner, 0), rows, 0, 4))
    add_up(step, by_g, column_sums(column_blocks(place, acts, partner, 1), rows, 4, 2))

    @pl.when(step == pl.num_programs(0) - 1)
    def _():
        kept[:1280] = by_x[:, :128]
        kept[1280:] = by_g[:, :128]
        away[:1280] = by_x[:, 128:]
        away[1280:] = by_g[:, 128:]


def term_kernel(example, kept, got, across, act, factor, dh, mask, out):
    rows = lax.broadcasted_iota(jnp.int32, (8, 128), 0)
    lanes = lax.broadcasted_iota(jnp.int32, (8, 128), 1)
    total = jnp.zeros((8, 128), F32)
    for k in range(2):

        def summed(at):
            part = slice(at * 320, (at + 1) * 320)
            return kept[part] + got[part]

        tangent = (factor[...] * summed(k) + act[...] * summed(2 + k)).astype(BF16)
        value = tangent.astype(F32) * dh[...]
        value += across[...].astype(F32) * summed(4 + k)
        value = jnp.sum(value, axis=0, keepdims=True) * mask[...]
        value = jnp.sum(value, axis=1, keepdims=True)
        total = jnp.where((rows == example[0]) & (lanes == k), value, total)
    out[...] = total


def whole(shape):
    return pl.BlockSpec(shape, lambda s, p: (0,) * len(shape))


def weight_spec(count):
    return pl.BlockSpec((2, 1, 2, count, 320, 256), lambda s, p: (0, s, 0, 0, 0, 0))


def column_spec(other):
    def index(s, p):
        return ((jnp.bitwise_xor(p[0], other) * 2 + s - p[3] + 4) % 4, 0, 0, 0)

    return pl.BlockSpec((1, 6, 320, 256), index)


def shards(tokens, out_grad, loss_mask, w_in0, w_in1, w_out, tan_in0, tan_in1, tan_out):
    fsdp = lax.axis_index("fsdp")
    seq = lax.axis_index("seq")
    rows = tokens.shape[0]
    length = rows * lax.axis_size("seq") // EXAMPLES
    place = jnp.stack(
        [fsdp // 16, fsdp % 4, seq * rows // length, seq // 4, seq // 2 % 2, seq % 2]
    ).astype(jnp.int32)

    stack_w = jnp.stack([w_in0, w_in1, w_out])
    both = jnp.stack([tokens, out_grad])
    other = lax.ppermute(both, "fsdp", [(i, (i + 16) % 32) for i in range(32)])
    _, _, tan_in0, tan_in1, tan_out = lax.optimization_barrier(
        (stack_w, other, tan_in0, tan_in1, tan_out)
    )
    stack_t = jnp.concatenate([tan_in0, tan_in1, tan_out], axis=0)
    full_w = lax.all_gather(stack_w, "seq", axis=0).reshape(2, 4, 2, 3, 320, 256)

    t_plus, t_minus = y_shift(stack_t, 1), y_shift(stack_t, -1)

    both = jnp.stack([both, other])
    far = [both] + [z_shift(both, step) for step in (4, 8, 12)]
    z_hi = fsdp // 4 % 4
    own = lax.dynamic_slice_in_dim(jnp.stack(far + far[:3]), (4 - z_hi) % 4, 4, axis=0)
    plus = z_shift(own, 1)
    minus = z_shift(own, -1)
    two_x = z_shift(own[:, :, 0], 2)
    two_g = z_shift(own[:, :, 1], -2)
    acts = jnp.stack([own, plus, jnp.stack([two_x, two_g], axis=2), minus], axis=3)

    half_plus, half_minus, _ = lax.optimization_barrier((t_plus[:3], t_minus[3:], own))
    half_plus, half_minus = y_shift(half_plus, 1), y_shift(half_minus, -1)
    half_plus, half_minus, _ = lax.optimization_barrier((half_plus, half_minus, acts))
    t_two = jnp.concatenate([half_plus, half_minus], axis=0)
    mine = jnp.stack([stack_t, t_plus, t_two, t_minus])
    theirs = lax.ppermute(mine, "seq", [(i, i ^ 1) for i in range(16)])

    partner = lax.dynamic_index_in_dim(
        acts.reshape((2, 2) + acts.shape[1:]), 1 - seq // 2 % 2, 1, False
    )
    partner = lax.ppermute(partner, "seq", [(i, i ^ 2) for i in range(16)])

    flat = jax.ShapeDtypeStruct((320, 128), F32)
    hidden, across, act, factor, dh = pl.pallas_call(
        primal_kernel,
        out_shape=(
            jax.ShapeDtypeStruct((128, 320), BF16),
            jax.ShapeDtypeStruct((320, 128), BF16),
            flat,
            flat,
            flat,
        ),
        grid_spec=pltpu.PrefetchScalarGridSpec(
            num_scalar_prefetch=1,
            grid=(4,),
            in_specs=[
                pl.BlockSpec((1, 2, 2, 4, 128, 128), lambda s, p: (s, 0, 0, 0, 0, 0)),
                weight_spec(3),
            ],
            out_specs=(whole((128, 320)),) + (whole((320, 128)),) * 4,
            scratch_shapes=[pltpu.VMEM((640, 128), F32), pltpu.VMEM((320, 128), F32)],
        ),
        compiler_params=pltpu.CompilerParams(vmem_limit_bytes=32 * 2**20),
        cost_estimate=pl.CostEstimate(
            flops=2 * 3 * 128 * 320 * 4096, bytes_accessed=10 * 2**20, transcendentals=40960
        ),
        name="primal",
    )(place, acts, full_w)

    by_x_hi = pl.BlockSpec((1, 4, 128, 128), lambda s, p: (s, 0, 0, 0))
    half_sums = jax.ShapeDtypeStruct((4, 128, 128), F32)
    both_sums = jax.ShapeDtypeStruct((2, 4, 128, 128), F32)
    kept, up, down, two_up, two_down = pl.pallas_call(
        output_kernel,
        out_shape=(both_sums, both_sums, both_sums, half_sums, half_sums),
        grid_spec=pltpu.PrefetchScalarGridSpec(
            num_scalar_prefetch=1,
            grid=(2,),
            in_specs=[
                whole((128, 320)),
                pl.BlockSpec(
                    (1, 4, 2, 1, 320, 256),
                    lambda s, p: (jnp.bitwise_xor(p[0], s), 0, 0, 2, 0, 0),
                ),
            ],
            out_specs=(by_x_hi, by_x_hi, by_x_hi, whole((4, 128, 128)), whole((4, 128, 128))),
        ),
        compiler_params=pltpu.CompilerParams(vmem_limit_bytes=32 * 2**20),
        cost_estimate=pl.CostEstimate(
            flops=2 * 128 * 320 * 4096, bytes_accessed=5 * 2**20, transcendentals=0
        ),
        name="block_sums",
    )(place, hidden, full_w)

    up = z_shift(up, -1)
    down = z_shift(down, 1)
    two_up = z_shift(two_up, -2)
    two_down = z_shift(two_down, 2)
    away = kept[1] + up[1] + down[1] + two_down
    away = lax.ppermute(away, "fsdp", [(i, (i + 16) % 32) for i in range(32)])
    partial = kept[0] + up[0] + down[0] + two_up + away
    partial = jnp.sum(lax.all_to_all(partial, "fsdp", 0, 0, axis_index_groups=Z_FAR), axis=0)
    block_out = partial.astype(BF16)

    partner, _ = lax.optimization_barrier((partner, kept))
    tall = jax.ShapeDtypeStruct((1920, 128), F32)
    in_column, to_send = pl.pallas_call(
        column_kernel,
        out_shape=(tall, tall),
        grid_spec=pltpu.PrefetchScalarGridSpec(
            num_scalar_prefetch=1,
            grid=(2,),
            in_specs=[
                pl.BlockSpec(
                    (1, 2, 2, 4, 128, 128), lambda s, p: (2 * s + p[4], 0, 0, 0, 0, 0)
                ),
                pl.BlockSpec((1, 2, 2, 4, 128, 128), lambda s, p: (s, 0, 0, 0, 0, 0)),
                column_spec(0),
                column_spec(0),
                column_spec(1),
                column_spec(1),
            ],
            out_specs=(whole((1920, 128)), whole((1920, 128))),
            scratch_shapes=[pltpu.VMEM((1280, 256), F32), pltpu.VMEM((640, 256), F32)],
        ),
        compiler_params=pltpu.CompilerParams(vmem_limit_bytes=32 * 2**20),
        cost_estimate=pl.CostEstimate(
            flops=2 * 6 * 128 * 320 * 4096, bytes_accessed=12 * 2**20, transcendentals=0
        ),
        name="column",
    )(place, acts, partner, mine, theirs, mine, theirs)
    got = lax.ppermute(to_send, "seq", [(i, i ^ 2) for i in range(16)])

    terms = pl.pallas_call(
        term_kernel,
        out_shape=jax.ShapeDtypeStruct((8, 128), F32),
        in_specs=[pl.BlockSpec(memory_space=pltpu.SMEM)]
        + [pl.BlockSpec(memory_space=pltpu.VMEM)] * 7,
        out_specs=pl.BlockSpec(memory_space=pltpu.VMEM),
        cost_estimate=pl.CostEstimate(
            flops=2**20, bytes_accessed=3 * 2**20, transcendentals=0
        ),
        compiler_params=pltpu.CompilerParams(vmem_limit_bytes=16 * 2**20),
        name="terms",
    )(place[2:3], in_column, got, across, act, factor, dh, loss_mask.astype(F32)[None])

    for axis, size, groups in (("seq", 16, None), ("fsdp", 16, Z_ALL), ("fsdp", 2, X_PAIRS)):
        copies = jnp.broadcast_to(terms[None], (size,) + terms.shape)
        terms = jnp.sum(lax.all_to_all(copies, axis, 0, 0, axis_index_groups=groups), axis=0)
        if axis == "seq":
            terms, block_out = lax.optimization_barrier((terms, block_out))
    return (block_out, terms[:EXAMPLES, :2])


def solution(mesh):
    placed = (
        P("seq", "fsdp"),
        P("seq", "fsdp"),
        P("seq"),
        P("fsdp", "seq"),
        P("fsdp", "seq"),
        P("fsdp", "seq"),
        P(None, "fsdp", "seq"),
        P(None, "fsdp", "seq"),
        P(None, "fsdp", "seq"),
    )
    return jax.shard_map(
        shards, mesh=mesh, in_specs=placed, out_specs=(P("seq", "fsdp"), P()), check_vma=False
    )
```

```python
import functools
import math

import jax
import jax.numpy as jnp
from jax import lax
from jax.experimental import pallas as pl
from jax.experimental.pallas import tpu as pltpu
from jax.sharding import PartitionSpec as P

EXAMPLES = 4
F32 = jnp.float32
BF16 = jnp.bfloat16
NT = (((1,), (1,)), ((), ()))

Z_FAR = [[h * 16 + q * 4 + r for q in range(4)] for h in range(2) for r in range(4)]
X_AND_NEAR = [[h * 16 + q * 4 + r for h in range(2) for r in range(4)] for q in range(4)]


def gelu_value_slope(value):
    coeff = math.sqrt(2.0 / math.pi)
    inner = coeff * (value + 0.044715 * value * value * value)
    tangent = jnp.tanh(inner)
    act = 0.5 * value * (1.0 + tangent)
    slope = 0.5 * (1.0 + tangent) + 0.5 * value * (1.0 - tangent * tangent) * coeff * (
        1.0 + 3.0 * 0.044715 * value * value
    )
    return (act, slope)


def z_shift(array, step):
    perm = [(h * 16 + (z + step) % 16, h * 16 + z) for h in range(2) for z in range(16)]
    return lax.ppermute(array, "fsdp", perm)


def y_shift(array, step):
    return lax.ppermute(array, "seq", [((i + 4 * step) % 16, i) for i in range(16)])


def pairs(place, acts, which):
    x_hi, z_lo = place[0], place[1]
    found = []
    for other in range(2):
        near = []
        for at in range(4):
            block = acts[0, other, which, 0]
            for shift in range(1, 4):
                block = jnp.where((z_lo + shift) % 4 == at, acts[0, other, which, shift], block)
            near.append(block)
        row = jnp.bitwise_xor(x_hi, other)
        for half in range(2):
            block = jnp.concatenate([near[2 * half], near[2 * half + 1]], axis=1)
            found.append((row, half, block))
    return found


def contract(blocks, weights, first, count):
    total = None
    for row, half, block in blocks:
        rows = weights[row, 0, half, first : first + count].reshape(count * 320, 256)
        term = lax.dot_general(rows, block, NT, preferred_element_type=F32)
        total = term if total is None else total + term
    return total


def add_up(step, sums, term):
    @pl.when(step == 0)
    def _():
        sums[...] = term

    @pl.when(step > 0)
    def _():
        sums[...] += term


def primal_kernel(place, acts, weights, mask, hidden, factors, by_x, by_g):
    step = pl.program_id(0)
    add_up(step, by_x, contract(pairs(place, acts, 0), weights, 0, 2))
    add_up(step, by_g, contract(pairs(place, acts, 1), weights, 2, 1))

    @pl.when(step == pl.num_programs(0) - 1)
    def _():
        upper = by_x[320:]
        act, slope = gelu_value_slope(by_x[:320])
        product = act * upper
        hidden[...] = jnp.transpose(product).astype(BF16)
        counted = by_g[...] * mask[...]
        factors[:320] = slope * upper * counted
        factors[320:640] = act * counted
        factors[640:] = product.astype(BF16).astype(F32) * mask[...]


def output_kernel(place, hidden, weights, own, plus, minus, two_a, two_b):
    z_lo = place[1]
    for z_hi in range(4):
        for shift in range(4):
            near = (z_lo + shift) % 4
            lanes = pl.ds(pl.multiple_of((near % 2) * 128, 128), 128)
            rows = weights[0, z_hi, near // 2, 0, :, lanes]
            value = jnp.dot(hidden[...], rows, preferred_element_type=F32)
            if shift == 0:
                own[0, z_hi] = value
            elif shift == 1:
                plus[0, z_hi] = value
            elif shift == 3:
                minus[0, z_hi] = value
            else:

                @pl.when(pl.program_id(0) == 0)
                def _():
                    two_a[z_hi] = value

                @pl.when(pl.program_id(0) == 1)
                def _():
                    two_b[z_hi] = value


def column_blocks(place, acts, partner, which):
    own = pairs(place, acts, which)
    theirs = pairs(place, partner, which)
    both = [jnp.concatenate([a[2], b[2]], axis=0) for a, b in zip(own, theirs)]
    found = []
    for other in range(2):
        low, high = both[2 * other], both[2 * other + 1]
        found.append(jnp.where(place[5] == 0, low, high))
        found.append(jnp.where(place[5] == 0, high, low))
    return found


def column_sums(blocks, rows, first, count):
    total = None
    for ref, block in zip(rows, blocks):
        part = ref[0, first : first + count].reshape(count * 320, 256)
        term = lax.dot_general(part, block, NT, preferred_element_type=F32)
        total = term if total is None else total + term
    return total


def column_kernel(
    place, acts, partner, mine_0, theirs_0, mine_1, theirs_1, own, their, out, by_x, by_g
):
    step = pl.program_id(0)
    rows = (mine_0, theirs_0, mine_1, theirs_1)
    add_up(step, by_x, column_sums(column_blocks(place, acts, partner, 0), rows, 0, 4))
    add_up(step, by_g, column_sums(column_blocks(place, acts, partner, 1), rows, 4, 2))

    @pl.when(step == pl.num_programs(0) - 1)
    def _():
        sublanes = lax.broadcasted_iota(jnp.int32, (8, 128), 0)
        lanes = lax.broadcasted_iota(jnp.int32, (8, 128), 1)
        total = jnp.zeros((8, 128), F32)
        for k in range(2):
            value = jnp.zeros((320, 128), F32)
            for factors, at in ((own, 0), (their, 128)):
                tokens = slice(at, at + 128)
                gate = by_x[k * 320 : (k + 1) * 320, tokens]
                upper = by_x[(2 + k) * 320 : (3 + k) * 320, tokens]
                value += factors[:320] * gate + factors[320:640] * upper
                value += factors[640:] * by_g[k * 320 : (k + 1) * 320, tokens]
            value = jnp.sum(value, axis=0, keepdims=True)
            value = jnp.sum(value, axis=1, keepdims=True)
            total = jnp.where((sublanes == place[2]) & (lanes == k), value, total)
        out[...] = total


def whole(shape):
    return pl.BlockSpec(shape, lambda s, p: (0,) * len(shape))


def weight_spec(count):
    return pl.BlockSpec((2, 1, 2, count, 320, 256), lambda s, p: (0, s, 0, 0, 0, 0))


def column_spec(other):
    def index(s, p):
        return ((jnp.bitwise_xor(p[0], other) * 2 + s - p[3] + 4) % 4, 0, 0, 0)

    return pl.BlockSpec((1, 6, 320, 256), index)


def shards(tokens, out_grad, loss_mask, w_in0, w_in1, w_out, tan_in0, tan_in1, tan_out):
    fsdp = lax.axis_index("fsdp")
    seq = lax.axis_index("seq")
    rows = tokens.shape[0]
    length = rows * lax.axis_size("seq") // EXAMPLES
    place = jnp.stack(
        [fsdp // 16, fsdp % 4, seq * rows // length, seq // 4, seq // 2 % 2, seq % 2]
    ).astype(jnp.int32)

    stack_w = jnp.stack([w_in0, w_in1, w_out])
    both = jnp.stack([tokens, out_grad])
    other = lax.ppermute(both, "fsdp", [(i, (i + 16) % 32) for i in range(32)])
    _, _, tan_in0, tan_in1, tan_out = lax.optimization_barrier(
        (stack_w, other, tan_in0, tan_in1, tan_out)
    )
    stack_t = jnp.concatenate([tan_in0, tan_in1, tan_out], axis=0)
    full_w = lax.all_gather(stack_w, "seq", axis=0).reshape(2, 4, 2, 3, 320, 256)

    t_plus, t_minus = y_shift(stack_t, 1), y_shift(stack_t, -1)

    both = jnp.stack([both, other])
    far = [both] + [z_shift(both, step) for step in (4, 8, 12)]
    z_hi = fsdp // 4 % 4
    own = lax.dynamic_slice_in_dim(jnp.stack(far + far[:3]), (4 - z_hi) % 4, 4, axis=0)
    plus = z_shift(own, 1)
    minus = z_shift(own, -1)
    two_x = z_shift(own[:, :, 0], 2)
    two_g = z_shift(own[:, :, 1], -2)
    acts = jnp.stack([own, plus, jnp.stack([two_x, two_g], axis=2), minus], axis=3)

    half_plus, half_minus, _ = lax.optimization_barrier((t_plus[:3], t_minus[3:], acts))
    half_plus, half_minus = y_shift(half_plus, 1), y_shift(half_minus, -1)

    partner = lax.dynamic_index_in_dim(
        acts.reshape((2, 2) + acts.shape[1:]), 1 - seq // 2 % 2, 1, False
    )
    partner = lax.ppermute(partner, "seq", [(i, i ^ 2) for i in range(16)])

    hidden, factors = pl.pallas_call(
        primal_kernel,
        out_shape=(
            jax.ShapeDtypeStruct((128, 320), BF16),
            jax.ShapeDtypeStruct((960, 128), F32),
        ),
        grid_spec=pltpu.PrefetchScalarGridSpec(
            num_scalar_prefetch=1,
            grid=(4,),
            in_specs=[
                pl.BlockSpec((1, 2, 2, 4, 128, 128), lambda s, p: (s, 0, 0, 0, 0, 0)),
                weight_spec(3),
                whole((1, 128)),
            ],
            out_specs=(whole((128, 320)), whole((960, 128))),
            scratch_shapes=[pltpu.VMEM((640, 128), F32), pltpu.VMEM((320, 128), F32)],
        ),
        compiler_params=pltpu.CompilerParams(vmem_limit_bytes=32 * 2**20),
        cost_estimate=pl.CostEstimate(
            flops=2 * 3 * 128 * 320 * 4096, bytes_accessed=10 * 2**20, transcendentals=40960
        ),
        name="primal",
    )(place, acts, full_w, loss_mask.astype(F32)[None])
    their = lax.ppermute(factors, "seq", [(i, i ^ 2) for i in range(16)])

    by_x_hi = pl.BlockSpec((1, 4, 128, 128), lambda s, p: (s, 0, 0, 0))
    half_sums = jax.ShapeDtypeStruct((4, 128, 128), F32)
    both_sums = jax.ShapeDtypeStruct((2, 4, 128, 128), F32)
    kept, up, down, two_up, two_down = pl.pallas_call(
        output_kernel,
        out_shape=(both_sums, both_sums, both_sums, half_sums, half_sums),
        grid_spec=pltpu.PrefetchScalarGridSpec(
            num_scalar_prefetch=1,
            grid=(2,),
            in_specs=[
                whole((128, 320)),
                pl.BlockSpec(
                    (1, 4, 2, 1, 320, 256),
                    lambda s, p: (jnp.bitwise_xor(p[0], s), 0, 0, 2, 0, 0),
                ),
            ],
            out_specs=(by_x_hi, by_x_hi, by_x_hi, whole((4, 128, 128)), whole((4, 128, 128))),
        ),
        compiler_params=pltpu.CompilerParams(vmem_limit_bytes=32 * 2**20),
        cost_estimate=pl.CostEstimate(
            flops=2 * 128 * 320 * 4096, bytes_accessed=5 * 2**20, transcendentals=0
        ),
        name="block_sums",
    )(place, hidden, full_w)

    half_plus, half_minus, _ = lax.optimization_barrier((half_plus, half_minus, kept))
    t_two = jnp.concatenate([half_plus, half_minus], axis=0)
    mine = jnp.stack([stack_t, t_plus, t_two, t_minus])
    theirs = lax.ppermute(mine, "seq", [(i, i ^ 1) for i in range(16)])

    up = z_shift(up, -1)
    down = z_shift(down, 1)
    two_up = z_shift(two_up, -2)
    two_down = z_shift(two_down, 2)
    away = kept[1] + up[1] + down[1] + two_down
    partner, _ = lax.optimization_barrier((partner, away))
    away = lax.ppermute(away, "fsdp", [(i, (i + 16) % 32) for i in range(32)])
    partial = kept[0] + up[0] + down[0] + two_up + away

    terms = pl.pallas_call(
        column_kernel,
        out_shape=jax.ShapeDtypeStruct((8, 128), F32),
        grid_spec=pltpu.PrefetchScalarGridSpec(
            num_scalar_prefetch=1,
            grid=(2,),
            in_specs=[
                pl.BlockSpec(
                    (1, 2, 2, 4, 128, 128), lambda s, p: (2 * s + p[4], 0, 0, 0, 0, 0)
                ),
                pl.BlockSpec((1, 2, 2, 4, 128, 128), lambda s, p: (s, 0, 0, 0, 0, 0)),
                column_spec(0),
                column_spec(0),
                column_spec(1),
                column_spec(1),
                whole((960, 128)),
                whole((960, 128)),
            ],
            out_specs=whole((8, 128)),
            scratch_shapes=[pltpu.VMEM((1280, 256), F32), pltpu.VMEM((640, 256), F32)],
        ),
        compiler_params=pltpu.CompilerParams(vmem_limit_bytes=32 * 2**20),
        cost_estimate=pl.CostEstimate(
            flops=2 * 6 * 128 * 320 * 4096, bytes_accessed=12 * 2**20, transcendentals=0
        ),
        name="column",
    )(place, acts, partner, mine, theirs, mine, theirs, factors, their)

    def sum_over(copies, axis, groups):
        return jnp.sum(lax.all_to_all(copies, axis, 0, 0, axis_index_groups=groups), axis=0)

    terms = sum_over(jnp.broadcast_to(terms[None], (16, 8, 128)), "seq", None)
    copies = jnp.broadcast_to(terms[None], (4, 8, 128))
    both = sum_over(jnp.concatenate([partial, copies], axis=1), "fsdp", Z_FAR)
    block_out = both[:128].astype(BF16)
    terms = sum_over(jnp.broadcast_to(both[None, 128:], (8, 8, 128)), "fsdp", X_AND_NEAR)
    return (block_out, terms[:EXAMPLES, :2])


def solution(mesh):
    placed = (
        P("seq", "fsdp"),
        P("seq", "fsdp"),
        P("seq"),
        P("fsdp", "seq"),
        P("fsdp", "seq"),
        P("fsdp", "seq"),
        P(None, "fsdp", "seq"),
        P(None, "fsdp", "seq"),
        P(None, "fsdp", "seq"),
    )
    return jax.shard_map(
        shards, mesh=mesh, in_specs=placed, out_specs=(P("seq", "fsdp"), P()), check_vma=False
    )
```

```python
import functools
import math

import jax
import jax.numpy as jnp
from jax import lax
from jax.experimental import pallas as pl
from jax.experimental.pallas import tpu as pltpu
from jax.sharding import PartitionSpec as P

EXAMPLES = 4
F32 = jnp.float32
BF16 = jnp.bfloat16
NT = (((1,), (1,)), ((), ()))

Z_FAR = [[h * 16 + q * 4 + r for q in range(4)] for h in range(2) for r in range(4)]
X_AND_NEAR = [[h * 16 + q * 4 + r for h in range(2) for r in range(4)] for q in range(4)]


def gelu_value_slope(value):
    coeff = math.sqrt(2.0 / math.pi)
    inner = coeff * (value + 0.044715 * value * value * value)
    tangent = jnp.tanh(inner)
    act = 0.5 * value * (1.0 + tangent)
    slope = 0.5 * (1.0 + tangent) + 0.5 * value * (1.0 - tangent * tangent) * coeff * (
        1.0 + 3.0 * 0.044715 * value * value
    )
    return (act, slope)


def z_shift(array, step):
    perm = [(h * 16 + (z + step) % 16, h * 16 + z) for h in range(2) for z in range(16)]
    return lax.ppermute(array, "fsdp", perm)


def y_shift(array, step):
    return lax.ppermute(array, "seq", [((i + 4 * step) % 16, i) for i in range(16)])


def pairs(place, acts, which):
    x_hi, z_lo = place[0], place[1]
    found = []
    for other in range(2):
        near = []
        for at in range(4):
            block = acts[0, other, which, 0]
            for shift in range(1, 4):
                block = jnp.where((z_lo + shift) % 4 == at, acts[0, other, which, shift], block)
            near.append(block)
        row = jnp.bitwise_xor(x_hi, other)
        for half in range(2):
            block = jnp.concatenate([near[2 * half], near[2 * half + 1]], axis=1)
            found.append((row, half, block))
    return found


def contract(blocks, weights, first, count):
    total = None
    for row, half, block in blocks:
        rows = weights[row, 0, half, first : first + count].reshape(count * 320, 256)
        term = lax.dot_general(rows, block, NT, preferred_element_type=F32)
        total = term if total is None else total + term
    return total


def add_up(step, sums, term):
    @pl.when(step == 0)
    def _():
        sums[...] = term

    @pl.when(step > 0)
    def _():
        sums[...] += term


def primal_kernel(place, acts, weights, mask, hidden, factors, by_x, by_g):
    step = pl.program_id(0)
    add_up(step, by_x, contract(pairs(place, acts, 0), weights, 0, 2))
    add_up(step, by_g, contract(pairs(place, acts, 1), weights, 2, 1))

    @pl.when(step == pl.num_programs(0) - 1)
    def _():
        upper = by_x[320:]
        act, slope = gelu_value_slope(by_x[:320])
        product = act * upper
        hidden[...] = jnp.transpose(product).astype(BF16)
        counted = by_g[...] * mask[...]
        factors[:320] = slope * upper * counted
        factors[320:640] = act * counted
        factors[640:] = product.astype(BF16).astype(F32) * mask[...]


def output_kernel(place, hidden, weights, own, plus, minus, two_a, two_b):
    z_lo = place[1]
    for z_hi in range(4):
        for shift in range(4):
            near = (z_lo + shift) % 4
            lanes = pl.ds(pl.multiple_of((near % 2) * 128, 128), 128)
            rows = weights[0, z_hi, near // 2, 0, :, lanes]
            value = jnp.dot(hidden[...], rows, preferred_element_type=F32)
            if shift == 0:
                own[0, z_hi] = value
            elif shift == 1:
                plus[0, z_hi] = value
            elif shift == 3:
                minus[0, z_hi] = value
            else:

                @pl.when(pl.program_id(0) == 0)
                def _():
                    two_a[z_hi] = value

                @pl.when(pl.program_id(0) == 1)
                def _():
                    two_b[z_hi] = value


def column_blocks(place, acts, partner, which):
    own = pairs(place, acts, which)
    theirs = pairs(place, partner, which)
    both = [jnp.concatenate([a[2], b[2]], axis=0) for a, b in zip(own, theirs)]
    found = []
    for other in range(2):
        low, high = both[2 * other], both[2 * other + 1]
        found.append(jnp.where(place[5] == 0, low, high))
        found.append(jnp.where(place[5] == 0, high, low))
    return found


def column_sums(blocks, rows, first, count):
    total = None
    for ref, block in zip(rows, blocks):
        part = ref[0, first : first + count].reshape(count * 320, 256)
        term = lax.dot_general(part, block, NT, preferred_element_type=F32)
        total = term if total is None else total + term
    return total


def column_kernel(
    place, acts, partner, mine_0, theirs_0, mine_1, theirs_1, own, their, out, by_x, by_g
):
    step = pl.program_id(0)
    rows = (mine_0, theirs_0, mine_1, theirs_1)
    add_up(step, by_x, column_sums(column_blocks(place, acts, partner, 0), rows, 0, 4))
    add_up(step, by_g, column_sums(column_blocks(place, acts, partner, 1), rows, 4, 2))

    @pl.when(step == pl.num_programs(0) - 1)
    def _():
        sublanes = lax.broadcasted_iota(jnp.int32, (8, 128), 0)
        lanes = lax.broadcasted_iota(jnp.int32, (8, 128), 1)
        total = jnp.zeros((8, 128), F32)
        for k in range(2):
            value = jnp.zeros((320, 128), F32)
            for factors, at in ((own, 0), (their, 128)):
                tokens = slice(at, at + 128)
                gate = by_x[k * 320 : (k + 1) * 320, tokens]
                upper = by_x[(2 + k) * 320 : (3 + k) * 320, tokens]
                value += factors[:320] * gate + factors[320:640] * upper
                value += factors[640:] * by_g[k * 320 : (k + 1) * 320, tokens]
            value = jnp.sum(value, axis=0, keepdims=True)
            value = jnp.sum(value, axis=1, keepdims=True)
            total = jnp.where((sublanes == place[2]) & (lanes == k), value, total)
        out[...] = total


def whole(shape):
    return pl.BlockSpec(shape, lambda s, p: (0,) * len(shape))


def weight_spec(count):
    return pl.BlockSpec((2, 1, 2, count, 320, 256), lambda s, p: (0, s, 0, 0, 0, 0))


def column_spec(other):
    def index(s, p):
        return ((jnp.bitwise_xor(p[0], other) * 2 + s - p[3] + 4) % 4, 0, 0, 0)

    return pl.BlockSpec((1, 6, 320, 256), index)


def shards(tokens, out_grad, loss_mask, w_in0, w_in1, w_out, tan_in0, tan_in1, tan_out):
    fsdp = lax.axis_index("fsdp")
    seq = lax.axis_index("seq")
    rows = tokens.shape[0]
    length = rows * lax.axis_size("seq") // EXAMPLES
    place = jnp.stack(
        [fsdp // 16, fsdp % 4, seq * rows // length, seq // 4, seq // 2 % 2, seq % 2]
    ).astype(jnp.int32)

    stack_w = jnp.stack([w_in0, w_in1, w_out])
    _, tan_in0, tan_in1, tan_out = lax.optimization_barrier(
        (stack_w, tan_in0, tan_in1, tan_out)
    )
    stack_t = jnp.concatenate([tan_in0, tan_in1, tan_out], axis=0)
    both = jnp.stack([tokens, out_grad])
    both, _ = lax.optimization_barrier((both, stack_t))
    other = lax.ppermute(both, "fsdp", [(i, (i + 16) % 32) for i in range(32)])
    full_w = lax.all_gather(stack_w, "seq", axis=0).reshape(2, 4, 2, 3, 320, 256)

    t_plus, t_minus = y_shift(stack_t, 1), y_shift(stack_t, -1)

    own = lax.all_gather(jnp.stack([both, other]), "fsdp", axis=0, axis_index_groups=Z_FAR)
    plus = z_shift(own, 1)
    minus = z_shift(own, -1)
    two_x = z_shift(own[:, :, 0], 2)
    two_g = z_shift(own[:, :, 1], -2)
    acts = jnp.stack([own, plus, jnp.stack([two_x, two_g], axis=2), minus], axis=3)

    t_plus, t_minus, _ = lax.optimization_barrier((t_plus, t_minus, own))
    half_plus, half_minus = y_shift(t_plus[:3], 1), y_shift(t_minus[3:], -1)

    partner = lax.dynamic_index_in_dim(
        acts.reshape((2, 2) + acts.shape[1:]), 1 - seq // 2 % 2, 1, False
    )
    partner = lax.ppermute(partner, "seq", [(i, i ^ 2) for i in range(16)])

    hidden, factors = pl.pallas_call(
        primal_kernel,
        out_shape=(
            jax.ShapeDtypeStruct((128, 320), BF16),
            jax.ShapeDtypeStruct((960, 128), F32),
        ),
        grid_spec=pltpu.PrefetchScalarGridSpec(
            num_scalar_prefetch=1,
            grid=(4,),
            in_specs=[
                pl.BlockSpec((1, 2, 2, 4, 128, 128), lambda s, p: (s, 0, 0, 0, 0, 0)),
                weight_spec(3),
                whole((1, 128)),
            ],
            out_specs=(whole((128, 320)), whole((960, 128))),
            scratch_shapes=[pltpu.VMEM((640, 128), F32), pltpu.VMEM((320, 128), F32)],
        ),
        compiler_params=pltpu.CompilerParams(vmem_limit_bytes=32 * 2**20),
        cost_estimate=pl.CostEstimate(
            flops=2 * 3 * 128 * 320 * 4096, bytes_accessed=10 * 2**20, transcendentals=40960
        ),
        name="primal",
    )(place, acts, full_w, loss_mask.astype(F32)[None])
    their = lax.ppermute(factors, "seq", [(i, i ^ 2) for i in range(16)])

    by_x_hi = pl.BlockSpec((1, 4, 128, 128), lambda s, p: (s, 0, 0, 0))
    half_sums = jax.ShapeDtypeStruct((4, 128, 128), F32)
    both_sums = jax.ShapeDtypeStruct((2, 4, 128, 128), F32)
    kept, up, down, two_up, two_down = pl.pallas_call(
        output_kernel,
        out_shape=(both_sums, both_sums, both_sums, half_sums, half_sums),
        grid_spec=pltpu.PrefetchScalarGridSpec(
            num_scalar_prefetch=1,
            grid=(2,),
            in_specs=[
                whole((128, 320)),
                pl.BlockSpec(
                    (1, 4, 2, 1, 320, 256),
                    lambda s, p: (jnp.bitwise_xor(p[0], s), 0, 0, 2, 0, 0),
                ),
            ],
            out_specs=(by_x_hi, by_x_hi, by_x_hi, whole((4, 128, 128)), whole((4, 128, 128))),
        ),
        compiler_params=pltpu.CompilerParams(vmem_limit_bytes=32 * 2**20),
        cost_estimate=pl.CostEstimate(
            flops=2 * 128 * 320 * 4096, bytes_accessed=5 * 2**20, transcendentals=0
        ),
        name="block_sums",
    )(place, hidden, full_w)

    half_plus, half_minus, *_ = lax.optimization_barrier(
        (half_plus, half_minus, plus, minus, two_x, two_g)
    )
    t_two = jnp.concatenate([half_plus, half_minus], axis=0)
    mine = jnp.stack([stack_t, t_plus, t_two, t_minus])
    theirs = lax.ppermute(mine, "seq", [(i, i ^ 1) for i in range(16)])

    up = z_shift(up, -1)
    down = z_shift(down, 1)
    two_up = z_shift(two_up, -2)
    two_down = z_shift(two_down, 2)
    away = kept[1] + up[1] + down[1] + two_down
    partner, _ = lax.optimization_barrier((partner, away))
    away = lax.ppermute(away, "fsdp", [(i, (i + 16) % 32) for i in range(32)])
    partial = kept[0] + up[0] + down[0] + two_up + away

    terms = pl.pallas_call(
        column_kernel,
        out_shape=jax.ShapeDtypeStruct((8, 128), F32),
        grid_spec=pltpu.PrefetchScalarGridSpec(
            num_scalar_prefetch=1,
            grid=(2,),
            in_specs=[
                pl.BlockSpec(
                    (1, 2, 2, 4, 128, 128), lambda s, p: (2 * s + p[4], 0, 0, 0, 0, 0)
                ),
                pl.BlockSpec((1, 2, 2, 4, 128, 128), lambda s, p: (s, 0, 0, 0, 0, 0)),
                column_spec(0),
                column_spec(0),
                column_spec(1),
                column_spec(1),
                whole((960, 128)),
                whole((960, 128)),
            ],
            out_specs=whole((8, 128)),
            scratch_shapes=[pltpu.VMEM((1280, 256), F32), pltpu.VMEM((640, 256), F32)],
        ),
        compiler_params=pltpu.CompilerParams(vmem_limit_bytes=32 * 2**20),
        cost_estimate=pl.CostEstimate(
            flops=2 * 6 * 128 * 320 * 4096, bytes_accessed=12 * 2**20, transcendentals=0
        ),
        name="column",
    )(place, acts, partner, mine, theirs, mine, theirs, factors, their)

    def sum_over(copies, axis, groups):
        return jnp.sum(lax.all_to_all(copies, axis, 0, 0, axis_index_groups=groups), axis=0)

    terms = sum_over(jnp.broadcast_to(terms[None], (16, 8, 128)), "seq", None)
    copies = jnp.broadcast_to(terms[None], (4, 8, 128))
    both = sum_over(jnp.concatenate([partial, copies], axis=1), "fsdp", Z_FAR)
    block_out = both[:128].astype(BF16)
    terms = sum_over(jnp.broadcast_to(both[None, 128:], (8, 8, 128)), "fsdp", X_AND_NEAR)
    return (block_out, terms[:EXAMPLES, :2])


def solution(mesh):
    placed = (
        P("seq", "fsdp"),
        P("seq", "fsdp"),
        P("seq"),
        P("fsdp", "seq"),
        P("fsdp", "seq"),
        P("fsdp", "seq"),
        P(None, "fsdp", "seq"),
        P(None, "fsdp", "seq"),
        P(None, "fsdp", "seq"),
    )
    return jax.shard_map(
        shards, mesh=mesh, in_specs=placed, out_specs=(P("seq", "fsdp"), P()), check_vma=False
    )
```

```python
import functools
import math

import jax
import jax.numpy as jnp
from jax import lax
from jax.experimental import pallas as pl
from jax.experimental.pallas import tpu as pltpu
from jax.sharding import PartitionSpec as P

EXAMPLES = 4
F32 = jnp.float32
BF16 = jnp.bfloat16
NT = (((1,), (1,)), ((), ()))

Z_FAR = [[h * 16 + q * 4 + r for q in range(4)] for h in range(2) for r in range(4)]
X_AND_NEAR = [[h * 16 + q * 4 + r for h in range(2) for r in range(4)] for q in range(4)]


def gelu_value_slope(value):
    coeff = math.sqrt(2.0 / math.pi)
    inner = coeff * (value + 0.044715 * value * value * value)
    tangent = jnp.tanh(inner)
    act = 0.5 * value * (1.0 + tangent)
    slope = 0.5 * (1.0 + tangent) + 0.5 * value * (1.0 - tangent * tangent) * coeff * (
        1.0 + 3.0 * 0.044715 * value * value
    )
    return (act, slope)


def z_shift(array, step):
    perm = [(h * 16 + (z + step) % 16, h * 16 + z) for h in range(2) for z in range(16)]
    return lax.ppermute(array, "fsdp", perm)


def y_shift(array, step):
    return lax.ppermute(array, "seq", [((i + 4 * step) % 16, i) for i in range(16)])


def pairs(place, acts, which):
    x_hi, z_lo = place[0], place[1]
    found = []
    for other in range(2):
        near = []
        for at in range(4):
            block = acts[0, other, which, 0]
            for shift in range(1, 4):
                block = jnp.where((z_lo + shift) % 4 == at, acts[0, other, which, shift], block)
            near.append(block)
        row = jnp.bitwise_xor(x_hi, other)
        for half in range(2):
            block = jnp.concatenate([near[2 * half], near[2 * half + 1]], axis=1)
            found.append((row, half, block))
    return found


def contract(blocks, weights, first, count):
    total = None
    for row, half, block in blocks:
        rows = weights[row, 0, half, first : first + count].reshape(count * 320, 256)
        term = lax.dot_general(rows, block, NT, preferred_element_type=F32)
        total = term if total is None else total + term
    return total


def add_up(step, sums, term):
    @pl.when(step == 0)
    def _():
        sums[...] = term

    @pl.when(step > 0)
    def _():
        sums[...] += term


def primal_kernel(place, acts, weights, mask, hidden, factors, by_x, by_g):
    step = pl.program_id(0)
    add_up(step, by_x, contract(pairs(place, acts, 0), weights, 0, 2))
    add_up(step, by_g, contract(pairs(place, acts, 1), weights, 2, 1))

    @pl.when(step == pl.num_programs(0) - 1)
    def _():
        upper = by_x[320:]
        act, slope = gelu_value_slope(by_x[:320])
        product = act * upper
        hidden[...] = jnp.transpose(product).astype(BF16)
        counted = by_g[...] * mask[...]
        factors[:320] = slope * upper * counted
        factors[320:640] = act * counted
        factors[640:] = product.astype(BF16).astype(F32) * mask[...]


def output_kernel(place, hidden, weights, own, plus, minus, two_a, two_b):
    z_lo = place[1]
    for z_hi in range(4):
        for shift in range(4):
            near = (z_lo + shift) % 4
            lanes = pl.ds(pl.multiple_of((near % 2) * 128, 128), 128)
            rows = weights[0, z_hi, near // 2, 0, :, lanes]
            value = jnp.dot(hidden[...], rows, preferred_element_type=F32)
            if shift == 0:
                own[0, z_hi] = value
            elif shift == 1:
                plus[0, z_hi] = value
            elif shift == 3:
                minus[0, z_hi] = value
            else:

                @pl.when(pl.program_id(0) == 0)
                def _():
                    two_a[z_hi] = value

                @pl.when(pl.program_id(0) == 1)
                def _():
                    two_b[z_hi] = value


def column_blocks(place, acts, partner, which):
    own = pairs(place, acts, which)
    theirs = pairs(place, partner, which)
    both = [jnp.concatenate([a[2], b[2]], axis=0) for a, b in zip(own, theirs)]
    found = []
    for other in range(2):
        low, high = both[2 * other], both[2 * other + 1]
        found.append(jnp.where(place[5] == 0, low, high))
        found.append(jnp.where(place[5] == 0, high, low))
    return found


def column_sums(blocks, rows, first, count):
    total = None
    for ref, block in zip(rows, blocks):
        part = ref[0, first : first + count].reshape(count * 320, 256)
        term = lax.dot_general(part, block, NT, preferred_element_type=F32)
        total = term if total is None else total + term
    return total


def column_kernel(
    place, acts, partner, mine_0, theirs_0, mine_1, theirs_1, own, their, out, by_x, by_g
):
    step = pl.program_id(0)
    rows = (mine_0, theirs_0, mine_1, theirs_1)
    add_up(step, by_x, column_sums(column_blocks(place, acts, partner, 0), rows, 0, 4))
    add_up(step, by_g, column_sums(column_blocks(place, acts, partner, 1), rows, 4, 2))

    @pl.when(step == pl.num_programs(0) - 1)
    def _():
        sublanes = lax.broadcasted_iota(jnp.int32, (8, 128), 0)
        lanes = lax.broadcasted_iota(jnp.int32, (8, 128), 1)
        total = jnp.zeros((8, 128), F32)
        for k in range(2):
            value = jnp.zeros((320, 128), F32)
            for factors, at in ((own, 0), (their, 128)):
                tokens = slice(at, at + 128)
                gate = by_x[k * 320 : (k + 1) * 320, tokens]
                upper = by_x[(2 + k) * 320 : (3 + k) * 320, tokens]
                value += factors[:320] * gate + factors[320:640] * upper
                value += factors[640:] * by_g[k * 320 : (k + 1) * 320, tokens]
            value = jnp.sum(value, axis=0, keepdims=True)
            value = jnp.sum(value, axis=1, keepdims=True)
            total = jnp.where((sublanes == place[2]) & (lanes == k), value, total)
        out[...] = total


def whole(shape):
    return pl.BlockSpec(shape, lambda s, p: (0,) * len(shape))


def weight_spec(count):
    return pl.BlockSpec((2, 1, 2, count, 320, 256), lambda s, p: (0, s, 0, 0, 0, 0))


def column_spec(other):
    def index(s, p):
        return ((jnp.bitwise_xor(p[0], other) * 2 + s - p[3] + 4) % 4, 0, 0, 0)

    return pl.BlockSpec((1, 6, 320, 256), index)


def shards(tokens, out_grad, loss_mask, w_in0, w_in1, w_out, tan_in0, tan_in1, tan_out):
    fsdp = lax.axis_index("fsdp")
    seq = lax.axis_index("seq")
    rows = tokens.shape[0]
    length = rows * lax.axis_size("seq") // EXAMPLES
    place = jnp.stack(
        [fsdp // 16, fsdp % 4, seq * rows // length, seq // 4, seq // 2 % 2, seq % 2]
    ).astype(jnp.int32)

    stack_w = jnp.stack([w_in0, w_in1, w_out])
    _, tan_in0, tan_in1, tan_out = lax.optimization_barrier(
        (stack_w, tan_in0, tan_in1, tan_out)
    )
    stack_t = jnp.concatenate([tan_in0, tan_in1, tan_out], axis=0)
    both = jnp.stack([tokens, out_grad])
    both, _ = lax.optimization_barrier((both, stack_t))
    other = lax.ppermute(both, "fsdp", [(i, (i + 16) % 32) for i in range(32)])
    full_w = lax.all_gather(stack_w, "seq", axis=0).reshape(2, 4, 2, 3, 320, 256)

    t_plus, t_minus = y_shift(stack_t, 1), y_shift(stack_t, -1)

    own = lax.all_gather(jnp.stack([both, other]), "fsdp", axis=0, axis_index_groups=Z_FAR)
    plus = z_shift(own, 1)
    minus = z_shift(own, -1)
    two_x = z_shift(own[:, :, 0], 2)
    two_g = z_shift(own[:, :, 1], -2)
    acts = jnp.stack([own, plus, jnp.stack([two_x, two_g], axis=2), minus], axis=3)

    t_plus, t_minus, _ = lax.optimization_barrier((t_plus, t_minus, own))
    half_plus, half_minus = y_shift(t_plus[:3], 1), y_shift(t_minus[3:], -1)

    partner = lax.dynamic_index_in_dim(
        acts.reshape((2, 2) + acts.shape[1:]), 1 - seq // 2 % 2, 1, False
    )
    partner = lax.ppermute(partner, "seq", [(i, i ^ 2) for i in range(16)])

    half_plus, half_minus, *_ = lax.optimization_barrier(
        (half_plus, half_minus, plus, minus, two_x, two_g)
    )
    t_two = jnp.concatenate([half_plus, half_minus], axis=0)
    mine = jnp.stack([stack_t, t_plus, t_two, t_minus])
    theirs = lax.ppermute(mine, "seq", [(i, i ^ 1) for i in range(16)])

    hidden, factors = pl.pallas_call(
        primal_kernel,
        out_shape=(
            jax.ShapeDtypeStruct((128, 320), BF16),
            jax.ShapeDtypeStruct((960, 128), F32),
        ),
        grid_spec=pltpu.PrefetchScalarGridSpec(
            num_scalar_prefetch=1,
            grid=(4,),
            in_specs=[
                pl.BlockSpec((1, 2, 2, 4, 128, 128), lambda s, p: (s, 0, 0, 0, 0, 0)),
                weight_spec(3),
                whole((1, 128)),
            ],
            out_specs=(whole((128, 320)), whole((960, 128))),
            scratch_shapes=[pltpu.VMEM((640, 128), F32), pltpu.VMEM((320, 128), F32)],
        ),
        compiler_params=pltpu.CompilerParams(vmem_limit_bytes=32 * 2**20),
        cost_estimate=pl.CostEstimate(
            flops=2 * 3 * 128 * 320 * 4096, bytes_accessed=10 * 2**20, transcendentals=40960
        ),
        name="primal",
    )(place, acts, full_w, loss_mask.astype(F32)[None])
    hidden, factors, theirs = lax.optimization_barrier((hidden, factors, theirs))
    their = lax.ppermute(factors, "seq", [(i, i ^ 2) for i in range(16)])

    by_x_hi = pl.BlockSpec((1, 4, 128, 128), lambda s, p: (s, 0, 0, 0))
    half_sums = jax.ShapeDtypeStruct((4, 128, 128), F32)
    both_sums = jax.ShapeDtypeStruct((2, 4, 128, 128), F32)
    kept, up, down, two_up, two_down = pl.pallas_call(
        output_kernel,
        out_shape=(both_sums, both_sums, both_sums, half_sums, half_sums),
        grid_spec=pltpu.PrefetchScalarGridSpec(
            num_scalar_prefetch=1,
            grid=(2,),
            in_specs=[
                whole((128, 320)),
                pl.BlockSpec(
                    (1, 4, 2, 1, 320, 256),
                    lambda s, p: (jnp.bitwise_xor(p[0], s), 0, 0, 2, 0, 0),
                ),
            ],
            out_specs=(by_x_hi, by_x_hi, by_x_hi, whole((4, 128, 128)), whole((4, 128, 128))),
        ),
        compiler_params=pltpu.CompilerParams(vmem_limit_bytes=32 * 2**20),
        cost_estimate=pl.CostEstimate(
            flops=2 * 128 * 320 * 4096, bytes_accessed=5 * 2**20, transcendentals=0
        ),
        name="block_sums",
    )(place, hidden, full_w)

    up = z_shift(up, -1)
    down = z_shift(down, 1)
    two_up = z_shift(two_up, -2)
    two_down = z_shift(two_down, 2)
    away = kept[1] + up[1] + down[1] + two_down
    partner, _ = lax.optimization_barrier((partner, kept))
    terms = pl.pallas_call(
        column_kernel,
        out_shape=jax.ShapeDtypeStruct((8, 128), F32),
        grid_spec=pltpu.PrefetchScalarGridSpec(
            num_scalar_prefetch=1,
            grid=(2,),
            in_specs=[
                pl.BlockSpec(
                    (1, 2, 2, 4, 128, 128), lambda s, p: (2 * s + p[4], 0, 0, 0, 0, 0)
                ),
                pl.BlockSpec((1, 2, 2, 4, 128, 128), lambda s, p: (s, 0, 0, 0, 0, 0)),
                column_spec(0),
                column_spec(0),
                column_spec(1),
                column_spec(1),
                whole((960, 128)),
                whole((960, 128)),
            ],
            out_specs=whole((8, 128)),
            scratch_shapes=[pltpu.VMEM((1280, 256), F32), pltpu.VMEM((640, 256), F32)],
        ),
        compiler_params=pltpu.CompilerParams(vmem_limit_bytes=32 * 2**20),
        cost_estimate=pl.CostEstimate(
            flops=2 * 6 * 128 * 320 * 4096, bytes_accessed=12 * 2**20, transcendentals=0
        ),
        name="column",
    )(place, acts, partner, mine, theirs, mine, theirs, factors, their)

    def sum_over(copies, axis, groups):
        return jnp.sum(lax.all_to_all(copies, axis, 0, 0, axis_index_groups=groups), axis=0)

    terms = sum_over(jnp.broadcast_to(terms[None], (16, 8, 128)), "seq", None)
    away, terms = lax.optimization_barrier((away, terms))
    away = lax.ppermute(away, "fsdp", [(i, (i + 16) % 32) for i in range(32)])
    partial = kept[0] + up[0] + down[0] + two_up + away
    copies = jnp.broadcast_to(terms[None], (4, 8, 128))
    both = sum_over(jnp.concatenate([partial, copies], axis=1), "fsdp", Z_FAR)
    block_out = both[:128].astype(BF16)
    terms = sum_over(jnp.broadcast_to(both[None, 128:], (8, 8, 128)), "fsdp", X_AND_NEAR)
    return (block_out, terms[:EXAMPLES, :2])


def solution(mesh):
    placed = (
        P("seq", "fsdp"),
        P("seq", "fsdp"),
        P("seq"),
        P("fsdp", "seq"),
        P("fsdp", "seq"),
        P("fsdp", "seq"),
        P(None, "fsdp", "seq"),
        P(None, "fsdp", "seq"),
        P(None, "fsdp", "seq"),
    )
    return jax.shard_map(
        shards, mesh=mesh, in_specs=placed, out_specs=(P("seq", "fsdp"), P()), check_vma=False
    )
```

```python
import functools
import math

import jax
import jax.numpy as jnp
from jax import lax
from jax.experimental import pallas as pl
from jax.experimental.pallas import tpu as pltpu
from jax.sharding import PartitionSpec as P

EXAMPLES = 4
F32 = jnp.float32
BF16 = jnp.bfloat16
NT = (((1,), (1,)), ((), ()))

Z_FAR = [[h * 16 + q * 4 + r for q in range(4)] for h in range(2) for r in range(4)]
Z_NEAR = [[h * 16 + q * 4 + r for r in range(4)] for h in range(2) for q in range(4)]


def gelu_value_slope(value):
    coeff = math.sqrt(2.0 / math.pi)
    inner = coeff * (value + 0.044715 * value * value * value)
    tangent = jnp.tanh(inner)
    act = 0.5 * value * (1.0 + tangent)
    slope = 0.5 * (1.0 + tangent) + 0.5 * value * (1.0 - tangent * tangent) * coeff * (
        1.0 + 3.0 * 0.044715 * value * value
    )
    return (act, slope)


def z_shift(array, step):
    perm = [(h * 16 + (z + step) % 16, h * 16 + z) for h in range(2) for z in range(16)]
    return lax.ppermute(array, "fsdp", perm)


def y_shift(array, step):
    return lax.ppermute(array, "seq", [((i + 4 * step) % 16, i) for i in range(16)])


def pairs(place, acts, which):
    x_hi, z_lo = place[0], place[1]
    found = []
    for other in range(2):
        near = []
        for at in range(4):
            block = acts[0, other, which, 0]
            for shift in range(1, 4):
                block = jnp.where((z_lo + shift) % 4 == at, acts[0, other, which, shift], block)
            near.append(block)
        row = jnp.bitwise_xor(x_hi, other)
        for half in range(2):
            block = jnp.concatenate([near[2 * half], near[2 * half + 1]], axis=1)
            found.append((row, half, block))
    return found


def contract(blocks, weights, first, count):
    total = None
    for row, half, block in blocks:
        rows = weights[row, 0, half, first : first + count].reshape(count * 320, 256)
        term = lax.dot_general(rows, block, NT, preferred_element_type=F32)
        total = term if total is None else total + term
    return total


def add_up(step, sums, term):
    @pl.when(step == 0)
    def _():
        sums[...] = term

    @pl.when(step > 0)
    def _():
        sums[...] += term


def primal_kernel(place, acts, weights, mask, hidden, factors, by_x, by_g):
    step = pl.program_id(0)
    add_up(step, by_x, contract(pairs(place, acts, 0), weights, 0, 2))
    add_up(step, by_g, contract(pairs(place, acts, 1), weights, 2, 1))

    @pl.when(step == pl.num_programs(0) - 1)
    def _():
        upper = by_x[320:]
        act, slope = gelu_value_slope(by_x[:320])
        product = act * upper
        hidden[...] = jnp.transpose(product).astype(BF16)
        counted = by_g[...] * mask[...]
        factors[:320] = slope * upper * counted
        factors[320:640] = act * counted
        factors[640:] = product.astype(BF16).astype(F32) * mask[...]


def output_kernel(place, hidden, weights, own, plus, minus, two_a, two_b):
    z_lo = place[1]
    for z_hi in range(4):
        for shift in range(4):
            near = (z_lo + shift) % 4
            lanes = pl.ds(pl.multiple_of((near % 2) * 128, 128), 128)
            rows = weights[0, z_hi, near // 2, 0, :, lanes]
            value = jnp.dot(hidden[...], rows, preferred_element_type=F32)
            if shift == 0:
                own[0, z_hi] = value
            elif shift == 1:
                plus[0, z_hi] = value
            elif shift == 3:
                minus[0, z_hi] = value
            else:

                @pl.when(pl.program_id(0) == 0)
                def _():
                    two_a[z_hi] = value

                @pl.when(pl.program_id(0) == 1)
                def _():
                    two_b[z_hi] = value


def column_blocks(place, acts, partner, which):
    own = pairs(place, acts, which)
    theirs = pairs(place, partner, which)
    both = [jnp.concatenate([a[2], b[2]], axis=0) for a, b in zip(own, theirs)]
    found = []
    for other in range(2):
        low, high = both[2 * other], both[2 * other + 1]
        found.append(jnp.where(place[5] == 0, low, high))
        found.append(jnp.where(place[5] == 0, high, low))
    return found


def column_sums(blocks, rows, first, count):
    total = None
    for ref, block in zip(rows, blocks):
        part = ref[0, first : first + count].reshape(count * 320, 256)
        term = lax.dot_general(part, block, NT, preferred_element_type=F32)
        total = term if total is None else total + term
    return total


def column_kernel(
    place, acts, partner, mine_0, theirs_0, mine_1, theirs_1, own, their, out, by_x, by_g
):
    step = pl.program_id(0)
    rows = (mine_0, theirs_0, mine_1, theirs_1)
    add_up(step, by_x, column_sums(column_blocks(place, acts, partner, 0), rows, 0, 4))
    add_up(step, by_g, column_sums(column_blocks(place, acts, partner, 1), rows, 4, 2))

    @pl.when(step == pl.num_programs(0) - 1)
    def _():
        sublanes = lax.broadcasted_iota(jnp.int32, (8, 128), 0)
        lanes = lax.broadcasted_iota(jnp.int32, (8, 128), 1)
        total = jnp.zeros((8, 128), F32)
        for k in range(2):
            value = jnp.zeros((320, 128), F32)
            for factors, at in ((own, 0), (their, 128)):
                tokens = slice(at, at + 128)
                gate = by_x[k * 320 : (k + 1) * 320, tokens]
                upper = by_x[(2 + k) * 320 : (3 + k) * 320, tokens]
                value += factors[:320] * gate + factors[320:640] * upper
                value += factors[640:] * by_g[k * 320 : (k + 1) * 320, tokens]
            value = jnp.sum(value, axis=0, keepdims=True)
            value = jnp.sum(value, axis=1, keepdims=True)
            total = jnp.where((sublanes == place[2]) & (lanes == k), value, total)
        out[...] = total


def whole(shape):
    return pl.BlockSpec(shape, lambda s, p: (0,) * len(shape))


def weight_spec(count):
    return pl.BlockSpec((2, 1, 2, count, 320, 256), lambda s, p: (0, s, 0, 0, 0, 0))


def column_spec(other):
    def index(s, p):
        return ((jnp.bitwise_xor(p[0], other) * 2 + s - p[3] + 4) % 4, 0, 0, 0)

    return pl.BlockSpec((1, 6, 320, 256), index)


def shards(tokens, out_grad, loss_mask, w_in0, w_in1, w_out, tan_in0, tan_in1, tan_out):
    fsdp = lax.axis_index("fsdp")
    seq = lax.axis_index("seq")
    rows = tokens.shape[0]
    length = rows * lax.axis_size("seq") // EXAMPLES
    place = jnp.stack(
        [fsdp // 16, fsdp % 4, seq * rows // length, seq // 4, seq // 2 % 2, seq % 2]
    ).astype(jnp.int32)

    stack_w = jnp.stack([w_in0, w_in1, w_out])
    _, tan_in0, tan_in1, tan_out = lax.optimization_barrier(
        (stack_w, tan_in0, tan_in1, tan_out)
    )
    stack_t = jnp.concatenate([tan_in0, tan_in1, tan_out], axis=0)
    both = jnp.stack([tokens, out_grad])
    both, _ = lax.optimization_barrier((both, stack_t))
    other = lax.ppermute(both, "fsdp", [(i, (i + 16) % 32) for i in range(32)])
    full_w = lax.all_gather(stack_w, "seq", axis=0).reshape(2, 4, 2, 3, 320, 256)

    t_plus, t_minus = y_shift(stack_t, 1), y_shift(stack_t, -1)

    own = lax.all_gather(jnp.stack([both, other]), "fsdp", axis=0, axis_index_groups=Z_FAR)
    plus = z_shift(own, 1)
    minus = z_shift(own, -1)
    two_x = z_shift(own[:, :, 0], 2)
    two_g = z_shift(own[:, :, 1], -2)
    acts = jnp.stack([own, plus, jnp.stack([two_x, two_g], axis=2), minus], axis=3)

    t_plus, t_minus, _ = lax.optimization_barrier((t_plus, t_minus, own))
    half_plus, half_minus = y_shift(t_plus[:3], 1), y_shift(t_minus[3:], -1)

    partner = lax.dynamic_index_in_dim(
        acts.reshape((2, 2) + acts.shape[1:]), 1 - seq // 2 % 2, 1, False
    )
    partner = lax.ppermute(partner, "seq", [(i, i ^ 2) for i in range(16)])

    half_plus, half_minus, *_ = lax.optimization_barrier(
        (half_plus, half_minus, plus, minus, two_x, two_g)
    )
    t_two = jnp.concatenate([half_plus, half_minus], axis=0)
    mine = jnp.stack([stack_t, t_plus, t_two, t_minus])
    theirs = lax.ppermute(mine, "seq", [(i, i ^ 1) for i in range(16)])

    hidden, factors = pl.pallas_call(
        primal_kernel,
        out_shape=(
            jax.ShapeDtypeStruct((128, 320), BF16),
            jax.ShapeDtypeStruct((960, 128), F32),
        ),
        grid_spec=pltpu.PrefetchScalarGridSpec(
            num_scalar_prefetch=1,
            grid=(4,),
            in_specs=[
                pl.BlockSpec((1, 2, 2, 4, 128, 128), lambda s, p: (s, 0, 0, 0, 0, 0)),
                weight_spec(3),
                whole((1, 128)),
            ],
            out_specs=(whole((128, 320)), whole((960, 128))),
            scratch_shapes=[pltpu.VMEM((640, 128), F32), pltpu.VMEM((320, 128), F32)],
        ),
        compiler_params=pltpu.CompilerParams(vmem_limit_bytes=32 * 2**20),
        cost_estimate=pl.CostEstimate(
            flops=2 * 3 * 128 * 320 * 4096, bytes_accessed=10 * 2**20, transcendentals=40960
        ),
        name="primal",
    )(place, acts, full_w, loss_mask.astype(F32)[None])
    hidden, factors, theirs = lax.optimization_barrier((hidden, factors, theirs))
    their = lax.ppermute(factors, "seq", [(i, i ^ 2) for i in range(16)])

    by_x_hi = pl.BlockSpec((1, 4, 128, 128), lambda s, p: (s, 0, 0, 0))
    half_sums = jax.ShapeDtypeStruct((4, 128, 128), F32)
    both_sums = jax.ShapeDtypeStruct((2, 4, 128, 128), F32)
    kept, up, down, two_up, two_down = pl.pallas_call(
        output_kernel,
        out_shape=(both_sums, both_sums, both_sums, half_sums, half_sums),
        grid_spec=pltpu.PrefetchScalarGridSpec(
            num_scalar_prefetch=1,
            grid=(2,),
            in_specs=[
                whole((128, 320)),
                pl.BlockSpec(
                    (1, 4, 2, 1, 320, 256),
                    lambda s, p: (jnp.bitwise_xor(p[0], s), 0, 0, 2, 0, 0),
                ),
            ],
            out_specs=(by_x_hi, by_x_hi, by_x_hi, whole((4, 128, 128)), whole((4, 128, 128))),
        ),
        compiler_params=pltpu.CompilerParams(vmem_limit_bytes=32 * 2**20),
        cost_estimate=pl.CostEstimate(
            flops=2 * 128 * 320 * 4096, bytes_accessed=5 * 2**20, transcendentals=0
        ),
        name="block_sums",
    )(place, hidden, full_w)

    up = z_shift(up, -1)
    down = z_shift(down, 1)
    two_up = z_shift(two_up, -2)
    two_down = z_shift(two_down, 2)
    away = kept[1] + up[1] + down[1] + two_down
    partner, _ = lax.optimization_barrier((partner, kept))
    terms = pl.pallas_call(
        column_kernel,
        out_shape=jax.ShapeDtypeStruct((8, 128), F32),
        grid_spec=pltpu.PrefetchScalarGridSpec(
            num_scalar_prefetch=1,
            grid=(2,),
            in_specs=[
                pl.BlockSpec(
                    (1, 2, 2, 4, 128, 128), lambda s, p: (2 * s + p[4], 0, 0, 0, 0, 0)
                ),
                pl.BlockSpec((1, 2, 2, 4, 128, 128), lambda s, p: (s, 0, 0, 0, 0, 0)),
                column_spec(0),
                column_spec(0),
                column_spec(1),
                column_spec(1),
                whole((960, 128)),
                whole((960, 128)),
            ],
            out_specs=whole((8, 128)),
            scratch_shapes=[pltpu.VMEM((1280, 256), F32), pltpu.VMEM((640, 256), F32)],
        ),
        compiler_params=pltpu.CompilerParams(vmem_limit_bytes=32 * 2**20),
        cost_estimate=pl.CostEstimate(
            flops=2 * 6 * 128 * 320 * 4096, bytes_accessed=12 * 2**20, transcendentals=0
        ),
        name="column",
    )(place, acts, partner, mine, theirs, mine, theirs, factors, their)

    def sum_over(copies, axis, groups):
        return jnp.sum(lax.all_to_all(copies, axis, 0, 0, axis_index_groups=groups), axis=0)

    terms = sum_over(jnp.broadcast_to(terms[None], (16, 8, 128)), "seq", None)
    away, terms, two_up = lax.optimization_barrier((away, terms, two_up))
    away = jnp.concatenate([away.reshape(512, 128), terms], axis=0)
    away = lax.ppermute(away, "fsdp", [(i, (i + 16) % 32) for i in range(32)])
    partial = kept[0] + up[0] + down[0] + two_up + away[:512].reshape(4, 128, 128)
    terms = terms + away[512:]
    copies = jnp.broadcast_to(terms[None], (4, 8, 128))
    both = sum_over(jnp.concatenate([partial, copies], axis=1), "fsdp", Z_FAR)
    block_out = both[:128].astype(BF16)
    terms = sum_over(jnp.broadcast_to(both[None, 128:], (4, 8, 128)), "fsdp", Z_NEAR)
    return (block_out, terms[:EXAMPLES, :2])


def solution(mesh):
    placed = (
        P("seq", "fsdp"),
        P("seq", "fsdp"),
        P("seq"),
        P("fsdp", "seq"),
        P("fsdp", "seq"),
        P("fsdp", "seq"),
        P(None, "fsdp", "seq"),
        P(None, "fsdp", "seq"),
        P(None, "fsdp", "seq"),
    )
    return jax.shard_map(
        shards, mesh=mesh, in_specs=placed, out_specs=(P("seq", "fsdp"), P()), check_vma=False
    )
```

```python
import functools
import math

import jax
import jax.numpy as jnp
from jax import lax
from jax.experimental import pallas as pl
from jax.experimental.pallas import tpu as pltpu
from jax.sharding import PartitionSpec as P

EXAMPLES = 4
F32 = jnp.float32
BF16 = jnp.bfloat16
NT = (((1,), (1,)), ((), ()))

Z_FAR = [[h * 16 + q * 4 + r for q in range(4)] for h in range(2) for r in range(4)]
Z_NEAR = [[h * 16 + q * 4 + r for r in range(4)] for h in range(2) for q in range(4)]


def gelu_value_slope(value):
    coeff = math.sqrt(2.0 / math.pi)
    inner = coeff * (value + 0.044715 * value * value * value)
    tangent = jnp.tanh(inner)
    act = 0.5 * value * (1.0 + tangent)
    slope = 0.5 * (1.0 + tangent) + 0.5 * value * (1.0 - tangent * tangent) * coeff * (
        1.0 + 3.0 * 0.044715 * value * value
    )
    return (act, slope)


def z_shift(array, step):
    perm = [(h * 16 + (z + step) % 16, h * 16 + z) for h in range(2) for z in range(16)]
    return lax.ppermute(array, "fsdp", perm)


def y_shift(array, step):
    return lax.ppermute(array, "seq", [((i + 4 * step) % 16, i) for i in range(16)])


def pairs(place, acts, which):
    x_hi, z_lo = place[0], place[1]
    found = []
    for other in range(2):
        near = []
        for at in range(4):
            block = acts[0, other, which, 0]
            for shift in range(1, 4):
                block = jnp.where((z_lo + shift) % 4 == at, acts[0, other, which, shift], block)
            near.append(block)
        row = jnp.bitwise_xor(x_hi, other)
        for half in range(2):
            block = jnp.concatenate([near[2 * half], near[2 * half + 1]], axis=1)
            found.append((row, half, block))
    return found


def contract(blocks, weights, first, count):
    total = None
    for row, half, block in blocks:
        rows = weights[row, 0, half, first : first + count].reshape(count * 320, 256)
        term = lax.dot_general(rows, block, NT, preferred_element_type=F32)
        total = term if total is None else total + term
    return total


def add_up(step, sums, term):
    @pl.when(step == 0)
    def _():
        sums[...] = term

    @pl.when(step > 0)
    def _():
        sums[...] += term


def primal_kernel(place, acts, weights, mask, hidden, factors, by_x, by_g):
    step = pl.program_id(0)
    add_up(step, by_x, contract(pairs(place, acts, 0), weights, 0, 2))
    add_up(step, by_g, contract(pairs(place, acts, 1), weights, 2, 1))

    @pl.when(step == pl.num_programs(0) - 1)
    def _():
        upper = by_x[320:]
        act, slope = gelu_value_slope(by_x[:320])
        product = act * upper
        hidden[...] = jnp.transpose(product).astype(BF16)
        counted = by_g[...] * mask[...]
        factors[:320] = slope * upper * counted
        factors[320:640] = act * counted
        factors[640:] = product.astype(BF16).astype(F32) * mask[...]


def output_kernel(place, hidden, weights, own, plus, minus, two_a, two_b):
    z_lo = place[1]
    for z_hi in range(4):
        for shift in range(4):
            near = (z_lo + shift) % 4
            lanes = pl.ds(pl.multiple_of((near % 2) * 128, 128), 128)
            rows = weights[0, z_hi, near // 2, 0, :, lanes]
            value = jnp.dot(hidden[...], rows, preferred_element_type=F32)
            if shift == 0:
                own[0, z_hi] = value
            elif shift == 1:
                plus[0, z_hi] = value
            elif shift == 3:
                minus[0, z_hi] = value
            else:

                @pl.when(pl.program_id(0) == 0)
                def _():
                    two_a[z_hi] = value

                @pl.when(pl.program_id(0) == 1)
                def _():
                    two_b[z_hi] = value


def column_blocks(place, acts, partner, which):
    own = pairs(place, acts, which)
    theirs = pairs(place, partner, which)
    both = [jnp.concatenate([a[2], b[2]], axis=0) for a, b in zip(own, theirs)]
    found = []
    for other in range(2):
        low, high = both[2 * other], both[2 * other + 1]
        found.append(jnp.where(place[5] == 0, low, high))
        found.append(jnp.where(place[5] == 0, high, low))
    return found


def column_sums(blocks, rows, first, count):
    total = None
    for ref, block in zip(rows, blocks):
        part = ref[0, first : first + count].reshape(count * 320, 256)
        term = lax.dot_general(part, block, NT, preferred_element_type=F32)
        total = term if total is None else total + term
    return total


def column_kernel(
    place, acts, partner, mine_0, theirs_0, mine_1, theirs_1, own, their, out, by_x, by_g
):
    step = pl.program_id(0)
    rows = (mine_0, theirs_0, mine_1, theirs_1)
    add_up(step, by_x, column_sums(column_blocks(place, acts, partner, 0), rows, 0, 4))
    add_up(step, by_g, column_sums(column_blocks(place, acts, partner, 1), rows, 4, 2))

    @pl.when(step == pl.num_programs(0) - 1)
    def _():
        sublanes = lax.broadcasted_iota(jnp.int32, (8, 128), 0)
        lanes = lax.broadcasted_iota(jnp.int32, (8, 128), 1)
        total = jnp.zeros((8, 128), F32)
        for k in range(2):
            value = jnp.zeros((320, 128), F32)
            for factors, at in ((own, 0), (their, 128)):
                tokens = slice(at, at + 128)
                gate = by_x[k * 320 : (k + 1) * 320, tokens]
                upper = by_x[(2 + k) * 320 : (3 + k) * 320, tokens]
                value += factors[:320] * gate + factors[320:640] * upper
                value += factors[640:] * by_g[k * 320 : (k + 1) * 320, tokens]
            value = jnp.sum(value, axis=0, keepdims=True)
            value = jnp.sum(value, axis=1, keepdims=True)
            total = jnp.where((sublanes == place[2]) & (lanes == k), value, total)
        out[...] = total


def whole(shape):
    return pl.BlockSpec(shape, lambda s, p: (0,) * len(shape))


def weight_spec(count):
    return pl.BlockSpec((2, 1, 2, count, 320, 256), lambda s, p: (0, s, 0, 0, 0, 0))


def column_spec(other):
    def index(s, p):
        return ((jnp.bitwise_xor(p[0], other) * 2 + s - p[3] + 4) % 4, 0, 0, 0)

    return pl.BlockSpec((1, 6, 320, 256), index)


def shards(tokens, out_grad, loss_mask, w_in0, w_in1, w_out, tan_in0, tan_in1, tan_out):
    fsdp = lax.axis_index("fsdp")
    seq = lax.axis_index("seq")
    rows = tokens.shape[0]
    length = rows * lax.axis_size("seq") // EXAMPLES
    place = jnp.stack(
        [fsdp // 16, fsdp % 4, seq * rows // length, seq // 4, seq // 2 % 2, seq % 2]
    ).astype(jnp.int32)

    stack_w = jnp.stack([w_in0, w_in1, w_out])
    _, tan_in0, tan_in1, tan_out = lax.optimization_barrier(
        (stack_w, tan_in0, tan_in1, tan_out)
    )
    stack_t = jnp.concatenate([tan_in0, tan_in1, tan_out], axis=0)
    both = jnp.stack([tokens, out_grad])
    both, _ = lax.optimization_barrier((both, stack_t))
    other = lax.ppermute(both, "fsdp", [(i, (i + 16) % 32) for i in range(32)])
    full_w = lax.all_gather(stack_w, "seq", axis=0).reshape(2, 4, 2, 3, 320, 256)

    t_plus, t_minus = y_shift(stack_t, 1), y_shift(stack_t, -1)

    own = lax.all_gather(jnp.stack([both, other]), "fsdp", axis=0, axis_index_groups=Z_FAR)
    plus = z_shift(own, 1)
    minus = z_shift(own, -1)
    two_x = z_shift(own[:, :, 0], 2)
    two_g = z_shift(own[:, :, 1], -2)
    acts = jnp.stack([own, plus, jnp.stack([two_x, two_g], axis=2), minus], axis=3)

    t_plus, t_minus, _ = lax.optimization_barrier((t_plus, t_minus, own))
    half_plus, half_minus = y_shift(t_plus[:3], 1), y_shift(t_minus[3:], -1)

    partner = lax.dynamic_index_in_dim(
        acts.reshape((2, 2) + acts.shape[1:]), 1 - seq // 2 % 2, 1, False
    )
    partner = lax.ppermute(partner, "seq", [(i, i ^ 2) for i in range(16)])

    half_plus, half_minus, *_ = lax.optimization_barrier(
        (half_plus, half_minus, plus, minus, two_x, two_g, full_w)
    )
    t_two = jnp.concatenate([half_plus, half_minus], axis=0)
    mine = jnp.stack([stack_t, t_plus, t_two, t_minus])
    theirs = lax.ppermute(mine, "seq", [(i, i ^ 1) for i in range(16)])

    hidden, factors = pl.pallas_call(
        primal_kernel,
        out_shape=(
            jax.ShapeDtypeStruct((128, 320), BF16),
            jax.ShapeDtypeStruct((960, 128), F32),
        ),
        grid_spec=pltpu.PrefetchScalarGridSpec(
            num_scalar_prefetch=1,
            grid=(4,),
            in_specs=[
                pl.BlockSpec((1, 2, 2, 4, 128, 128), lambda s, p: (s, 0, 0, 0, 0, 0)),
                weight_spec(3),
                whole((1, 128)),
            ],
            out_specs=(whole((128, 320)), whole((960, 128))),
            scratch_shapes=[pltpu.VMEM((640, 128), F32), pltpu.VMEM((320, 128), F32)],
        ),
        compiler_params=pltpu.CompilerParams(vmem_limit_bytes=32 * 2**20),
        cost_estimate=pl.CostEstimate(
            flops=2 * 3 * 128 * 320 * 4096, bytes_accessed=10 * 2**20, transcendentals=40960
        ),
        name="primal",
    )(place, acts, full_w, loss_mask.astype(F32)[None])
    hidden, factors, theirs = lax.optimization_barrier((hidden, factors, theirs))
    their = lax.ppermute(factors, "seq", [(i, i ^ 2) for i in range(16)])

    by_x_hi = pl.BlockSpec((1, 4, 128, 128), lambda s, p: (s, 0, 0, 0))
    half_sums = jax.ShapeDtypeStruct((4, 128, 128), F32)
    both_sums = jax.ShapeDtypeStruct((2, 4, 128, 128), F32)
    kept, up, down, two_up, two_down = pl.pallas_call(
        output_kernel,
        out_shape=(both_sums, both_sums, both_sums, half_sums, half_sums),
        grid_spec=pltpu.PrefetchScalarGridSpec(
            num_scalar_prefetch=1,
            grid=(2,),
            in_specs=[
                whole((128, 320)),
                pl.BlockSpec(
                    (1, 4, 2, 1, 320, 256),
                    lambda s, p: (jnp.bitwise_xor(p[0], s), 0, 0, 2, 0, 0),
                ),
            ],
            out_specs=(by_x_hi, by_x_hi, by_x_hi, whole((4, 128, 128)), whole((4, 128, 128))),
        ),
        compiler_params=pltpu.CompilerParams(vmem_limit_bytes=32 * 2**20),
        cost_estimate=pl.CostEstimate(
            flops=2 * 128 * 320 * 4096, bytes_accessed=5 * 2**20, transcendentals=0
        ),
        name="block_sums",
    )(place, hidden, full_w)

    up = z_shift(up, -1)
    down = z_shift(down, 1)
    two_up = z_shift(two_up, -2)
    two_down = z_shift(two_down, 2)
    away = kept[1] + up[1] + down[1] + two_down
    partner, _ = lax.optimization_barrier((partner, kept))
    terms = pl.pallas_call(
        column_kernel,
        out_shape=jax.ShapeDtypeStruct((8, 128), F32),
        grid_spec=pltpu.PrefetchScalarGridSpec(
            num_scalar_prefetch=1,
            grid=(2,),
            in_specs=[
                pl.BlockSpec(
                    (1, 2, 2, 4, 128, 128), lambda s, p: (2 * s + p[4], 0, 0, 0, 0, 0)
                ),
                pl.BlockSpec((1, 2, 2, 4, 128, 128), lambda s, p: (s, 0, 0, 0, 0, 0)),
                column_spec(0),
                column_spec(0),
                column_spec(1),
                column_spec(1),
                whole((960, 128)),
                whole((960, 128)),
            ],
            out_specs=whole((8, 128)),
            scratch_shapes=[pltpu.VMEM((1280, 256), F32), pltpu.VMEM((640, 256), F32)],
        ),
        compiler_params=pltpu.CompilerParams(vmem_limit_bytes=32 * 2**20),
        cost_estimate=pl.CostEstimate(
            flops=2 * 6 * 128 * 320 * 4096, bytes_accessed=12 * 2**20, transcendentals=0
        ),
        name="column",
    )(place, acts, partner, mine, theirs, mine, theirs, factors, their)

    def sum_over(copies, axis, groups):
        return jnp.sum(lax.all_to_all(copies, axis, 0, 0, axis_index_groups=groups), axis=0)

    terms = sum_over(jnp.broadcast_to(terms[None], (16, 8, 128)), "seq", None)
    away, terms, two_up = lax.optimization_barrier((away, terms, two_up))
    away = jnp.concatenate([away.reshape(512, 128), terms], axis=0)
    away = lax.ppermute(away, "fsdp", [(i, (i + 16) % 32) for i in range(32)])
    partial = kept[0] + up[0] + down[0] + two_up + away[:512].reshape(4, 128, 128)
    terms = terms + away[512:]
    for distance in (8, 4):
        side = fsdp % 16 // distance % 2
        count = distance // 4
        halves = partial.reshape(2, count * 128, 128)
        send = lax.dynamic_index_in_dim(halves, 1 - side, 0, False)
        swap = [(i, i ^ distance) for i in range(32)]
        got = lax.ppermute(jnp.concatenate([send, terms], axis=0), "fsdp", swap)
        partial = lax.dynamic_index_in_dim(halves, side, 0, False) + got[: count * 128]
        terms = terms + got[count * 128 :]
    block_out = partial.astype(BF16)
    terms = sum_over(jnp.broadcast_to(terms[None], (4, 8, 128)), "fsdp", Z_NEAR)
    return (block_out, terms[:EXAMPLES, :2])


def solution(mesh):
    placed = (
        P("seq", "fsdp"),
        P("seq", "fsdp"),
        P("seq"),
        P("fsdp", "seq"),
        P("fsdp", "seq"),
        P("fsdp", "seq"),
        P(None, "fsdp", "seq"),
        P(None, "fsdp", "seq"),
        P(None, "fsdp", "seq"),
    )
    return jax.shard_map(
        shards, mesh=mesh, in_specs=placed, out_specs=(P("seq", "fsdp"), P()), check_vma=False
    )
```

```python
import functools
import math

import jax
import jax.numpy as jnp
from jax import lax
from jax.experimental import pallas as pl
from jax.experimental.pallas import tpu as pltpu
from jax.sharding import PartitionSpec as P

EXAMPLES = 4
F32 = jnp.float32
BF16 = jnp.bfloat16
NT = (((1,), (1,)), ((), ()))

Z_FAR = [[h * 16 + q * 4 + r for q in range(4)] for h in range(2) for r in range(4)]
Z_NEAR = [[h * 16 + q * 4 + r for r in range(4)] for h in range(2) for q in range(4)]


def gelu_value_slope(value):
    coeff = math.sqrt(2.0 / math.pi)
    inner = coeff * (value + 0.044715 * value * value * value)
    tangent = jnp.tanh(inner)
    act = 0.5 * value * (1.0 + tangent)
    slope = 0.5 * (1.0 + tangent) + 0.5 * value * (1.0 - tangent * tangent) * coeff * (
        1.0 + 3.0 * 0.044715 * value * value
    )
    return (act, slope)


def z_shift(array, step):
    perm = [(h * 16 + (z + step) % 16, h * 16 + z) for h in range(2) for z in range(16)]
    return lax.ppermute(array, "fsdp", perm)


def y_shift(array, step):
    return lax.ppermute(array, "seq", [((i + 4 * step) % 16, i) for i in range(16)])


def pairs(place, acts, which):
    x_hi, z_lo = place[0], place[1]
    found = []
    for other in range(2):
        near = []
        for at in range(4):
            block = acts[0, other, which, 0]
            for shift in range(1, 4):
                block = jnp.where((z_lo + shift) % 4 == at, acts[0, other, which, shift], block)
            near.append(block)
        row = jnp.bitwise_xor(x_hi, other)
        for half in range(2):
            block = jnp.concatenate([near[2 * half], near[2 * half + 1]], axis=1)
            found.append((row, half, block))
    return found


def contract(blocks, weights, first, count):
    total = None
    for row, half, block in blocks:
        rows = weights[row, 0, half, first : first + count].reshape(count * 320, 256)
        term = lax.dot_general(rows, block, NT, preferred_element_type=F32)
        total = term if total is None else total + term
    return total


def add_up(step, sums, term):
    @pl.when(step == 0)
    def _():
        sums[...] = term

    @pl.when(step > 0)
    def _():
        sums[...] += term


def primal_kernel(place, acts, weights, mask, hidden, factors, by_x, by_g):
    step = pl.program_id(0)
    add_up(step, by_x, contract(pairs(place, acts, 0), weights, 0, 2))
    add_up(step, by_g, contract(pairs(place, acts, 1), weights, 2, 1))

    @pl.when(step == pl.num_programs(0) - 1)
    def _():
        upper = by_x[320:]
        act, slope = gelu_value_slope(by_x[:320])
        product = act * upper
        hidden[...] = jnp.transpose(product).astype(BF16)
        counted = by_g[...] * mask[...]
        factors[:320] = slope * upper * counted
        factors[320:640] = act * counted
        factors[640:] = product.astype(BF16).astype(F32) * mask[...]


def output_kernel(place, hidden, weights, own, plus, minus, two_a, two_b):
    z_lo = place[1]
    for z_hi in range(4):
        for shift in range(4):
            near = (z_lo + shift) % 4
            lanes = pl.ds(pl.multiple_of((near % 2) * 128, 128), 128)
            rows = weights[0, z_hi, near // 2, 0, :, lanes]
            value = jnp.dot(hidden[...], rows, preferred_element_type=F32)
            if shift == 0:
                own[0, z_hi] = value
            elif shift == 1:
                plus[0, z_hi] = value
            elif shift == 3:
                minus[0, z_hi] = value
            else:

                @pl.when(pl.program_id(0) == 0)
                def _():
                    two_a[z_hi] = value

                @pl.when(pl.program_id(0) == 1)
                def _():
                    two_b[z_hi] = value


def column_blocks(place, acts, partner, which):
    own = pairs(place, acts, which)
    theirs = pairs(place, partner, which)
    both = [jnp.concatenate([a[2], b[2]], axis=0) for a, b in zip(own, theirs)]
    found = []
    for other in range(2):
        low, high = both[2 * other], both[2 * other + 1]
        found.append(jnp.where(place[5] == 0, low, high))
        found.append(jnp.where(place[5] == 0, high, low))
    return found


def column_sums(blocks, rows, first, count):
    total = None
    for ref, block in zip(rows, blocks):
        part = ref[0, first : first + count].reshape(count * 320, 256)
        term = lax.dot_general(part, block, NT, preferred_element_type=F32)
        total = term if total is None else total + term
    return total


def column_kernel(
    place, acts, partner, mine_0, theirs_0, mine_1, theirs_1, own, their, out, by_x, by_g
):
    step = pl.program_id(0)
    rows = (mine_0, theirs_0, mine_1, theirs_1)
    add_up(step, by_x, column_sums(column_blocks(place, acts, partner, 0), rows, 0, 4))
    add_up(step, by_g, column_sums(column_blocks(place, acts, partner, 1), rows, 4, 2))

    @pl.when(step == pl.num_programs(0) - 1)
    def _():
        sublanes = lax.broadcasted_iota(jnp.int32, (8, 128), 0)
        lanes = lax.broadcasted_iota(jnp.int32, (8, 128), 1)
        total = jnp.zeros((8, 128), F32)
        for k in range(2):
            value = jnp.zeros((320, 128), F32)
            for factors, at in ((own, 0), (their, 128)):
                tokens = slice(at, at + 128)
                gate = by_x[k * 320 : (k + 1) * 320, tokens]
                upper = by_x[(2 + k) * 320 : (3 + k) * 320, tokens]
                value += factors[:320] * gate + factors[320:640] * upper
                value += factors[640:] * by_g[k * 320 : (k + 1) * 320, tokens]
            value = jnp.sum(value, axis=0, keepdims=True)
            value = jnp.sum(value, axis=1, keepdims=True)
            total = jnp.where((sublanes == place[2]) & (lanes == k), value, total)
        out[...] = total


def whole(shape):
    return pl.BlockSpec(shape, lambda s, p: (0,) * len(shape))


def weight_spec(count):
    return pl.BlockSpec((2, 1, 2, count, 320, 256), lambda s, p: (0, s, 0, 0, 0, 0))


def column_spec(other):
    def index(s, p):
        return ((jnp.bitwise_xor(p[0], other) * 2 + s - p[3] + 4) % 4, 0, 0, 0)

    return pl.BlockSpec((1, 6, 320, 256), index)


def shards(tokens, out_grad, loss_mask, w_in0, w_in1, w_out, tan_in0, tan_in1, tan_out):
    fsdp = lax.axis_index("fsdp")
    seq = lax.axis_index("seq")
    rows = tokens.shape[0]
    length = rows * lax.axis_size("seq") // EXAMPLES
    place = jnp.stack(
        [fsdp // 16, fsdp % 4, seq * rows // length, seq // 4, seq // 2 % 2, seq % 2]
    ).astype(jnp.int32)

    stack_w = jnp.stack([w_in0, w_in1, w_out])
    _, tan_in0, tan_in1, tan_out = lax.optimization_barrier(
        (stack_w, tan_in0, tan_in1, tan_out)
    )
    stack_t = jnp.concatenate([tan_in0, tan_in1, tan_out], axis=0)
    both = jnp.stack([tokens, out_grad])
    both, _ = lax.optimization_barrier((both, stack_t))
    other = lax.ppermute(both, "fsdp", [(i, (i + 16) % 32) for i in range(32)])
    full_w = lax.all_gather(stack_w, "seq", axis=0).reshape(2, 4, 2, 3, 320, 256)

    t_plus, t_minus = y_shift(stack_t, 1), y_shift(stack_t, -1)

    own = lax.all_gather(jnp.stack([both, other]), "fsdp", axis=0, axis_index_groups=Z_FAR)
    plus = z_shift(own, 1)
    minus = z_shift(own, -1)
    two_x = z_shift(own[:, :, 0], 2)
    two_g = z_shift(own[:, :, 1], -2)
    acts = jnp.stack([own, plus, jnp.stack([two_x, two_g], axis=2), minus], axis=3)

    t_plus, t_minus, _ = lax.optimization_barrier((t_plus, t_minus, own))
    half_plus, half_minus = y_shift(t_plus[:3], 1), y_shift(t_minus[3:], -1)

    partner = lax.dynamic_index_in_dim(
        acts.reshape((2, 2) + acts.shape[1:]), 1 - seq // 2 % 2, 1, False
    )
    partner = lax.ppermute(partner, "seq", [(i, i ^ 2) for i in range(16)])

    half_plus, half_minus, *_ = lax.optimization_barrier(
        (half_plus, half_minus, plus, minus, two_x, two_g)
    )
    t_two = jnp.concatenate([half_plus, half_minus], axis=0)
    mine = jnp.stack([stack_t, t_plus, t_two, t_minus])
    theirs = lax.ppermute(mine, "seq", [(i, i ^ 1) for i in range(16)])

    hidden, factors = pl.pallas_call(
        primal_kernel,
        out_shape=(
            jax.ShapeDtypeStruct((128, 320), BF16),
            jax.ShapeDtypeStruct((960, 128), F32),
        ),
        grid_spec=pltpu.PrefetchScalarGridSpec(
            num_scalar_prefetch=1,
            grid=(4,),
            in_specs=[
                pl.BlockSpec((1, 2, 2, 4, 128, 128), lambda s, p: (s, 0, 0, 0, 0, 0)),
                weight_spec(3),
                whole((1, 128)),
            ],
            out_specs=(whole((128, 320)), whole((960, 128))),
            scratch_shapes=[pltpu.VMEM((640, 128), F32), pltpu.VMEM((320, 128), F32)],
        ),
        compiler_params=pltpu.CompilerParams(vmem_limit_bytes=32 * 2**20),
        cost_estimate=pl.CostEstimate(
            flops=2 * 3 * 128 * 320 * 4096, bytes_accessed=10 * 2**20, transcendentals=40960
        ),
        name="primal",
    )(place, acts, full_w, loss_mask.astype(F32)[None])
    hidden, factors, theirs = lax.optimization_barrier((hidden, factors, theirs))
    their = lax.ppermute(factors, "seq", [(i, i ^ 2) for i in range(16)])

    by_x_hi = pl.BlockSpec((1, 4, 128, 128), lambda s, p: (s, 0, 0, 0))
    half_sums = jax.ShapeDtypeStruct((4, 128, 128), F32)
    both_sums = jax.ShapeDtypeStruct((2, 4, 128, 128), F32)
    kept, up, down, two_up, two_down = pl.pallas_call(
        output_kernel,
        out_shape=(both_sums, both_sums, both_sums, half_sums, half_sums),
        grid_spec=pltpu.PrefetchScalarGridSpec(
            num_scalar_prefetch=1,
            grid=(2,),
            in_specs=[
                whole((128, 320)),
                pl.BlockSpec(
                    (1, 4, 2, 1, 320, 256),
                    lambda s, p: (jnp.bitwise_xor(p[0], s), 0, 0, 2, 0, 0),
                ),
            ],
            out_specs=(by_x_hi, by_x_hi, by_x_hi, whole((4, 128, 128)), whole((4, 128, 128))),
        ),
        compiler_params=pltpu.CompilerParams(vmem_limit_bytes=32 * 2**20),
        cost_estimate=pl.CostEstimate(
            flops=2 * 128 * 320 * 4096, bytes_accessed=5 * 2**20, transcendentals=0
        ),
        name="block_sums",
    )(place, hidden, full_w)

    up = z_shift(up, -1)
    down = z_shift(down, 1)
    two_up = z_shift(two_up, -2)
    two_down = z_shift(two_down, 2)
    away = kept[1] + up[1] + down[1] + two_down
    partner, _ = lax.optimization_barrier((partner, kept))
    terms = pl.pallas_call(
        column_kernel,
        out_shape=jax.ShapeDtypeStruct((8, 128), F32),
        grid_spec=pltpu.PrefetchScalarGridSpec(
            num_scalar_prefetch=1,
            grid=(2,),
            in_specs=[
                pl.BlockSpec(
                    (1, 2, 2, 4, 128, 128), lambda s, p: (2 * s + p[4], 0, 0, 0, 0, 0)
                ),
                pl.BlockSpec((1, 2, 2, 4, 128, 128), lambda s, p: (s, 0, 0, 0, 0, 0)),
                column_spec(0),
                column_spec(0),
                column_spec(1),
                column_spec(1),
                whole((960, 128)),
                whole((960, 128)),
            ],
            out_specs=whole((8, 128)),
            scratch_shapes=[pltpu.VMEM((1280, 256), F32), pltpu.VMEM((640, 256), F32)],
        ),
        compiler_params=pltpu.CompilerParams(vmem_limit_bytes=32 * 2**20),
        cost_estimate=pl.CostEstimate(
            flops=2 * 6 * 128 * 320 * 4096, bytes_accessed=12 * 2**20, transcendentals=0
        ),
        name="column",
    )(place, acts, partner, mine, theirs, mine, theirs, factors, their)

    def sum_over(copies, axis, groups):
        return jnp.sum(lax.all_to_all(copies, axis, 0, 0, axis_index_groups=groups), axis=0)

    terms = sum_over(jnp.broadcast_to(terms[None], (16, 8, 128)), "seq", None)
    away, terms, two_up = lax.optimization_barrier((away, terms, two_up))
    away = jnp.concatenate([away.reshape(512, 128), terms], axis=0)
    away = lax.ppermute(away, "fsdp", [(i, (i + 16) % 32) for i in range(32)])
    partial = kept[0] + up[0] + down[0] + two_up + away[:512].reshape(4, 128, 128)
    terms = terms + away[512:]
    for distance in (8, 4):
        side = fsdp % 16 // distance % 2
        count = distance // 4
        halves = partial.reshape(2, count * 128, 128)
        send = lax.dynamic_index_in_dim(halves, 1 - side, 0, False)
        swap = [(i, i ^ distance) for i in range(32)]
        got = lax.ppermute(jnp.concatenate([send, terms], axis=0), "fsdp", swap)
        partial = lax.dynamic_index_in_dim(halves, side, 0, False) + got[: count * 128]
        terms = terms + got[count * 128 :]
    block_out = partial.astype(BF16)
    terms = sum_over(jnp.broadcast_to(terms[None], (4, 8, 128)), "fsdp", Z_NEAR)
    return (block_out, terms[:EXAMPLES, :2])


def solution(mesh):
    placed = (
        P("seq", "fsdp"),
        P("seq", "fsdp"),
        P("seq"),
        P("fsdp", "seq"),
        P("fsdp", "seq"),
        P("fsdp", "seq"),
        P(None, "fsdp", "seq"),
        P(None, "fsdp", "seq"),
        P(None, "fsdp", "seq"),
    )
    return jax.shard_map(
        shards, mesh=mesh, in_specs=placed, out_specs=(P("seq", "fsdp"), P()), check_vma=False
    )
```
